256 devices in a mesh: pb: 32 (over y, x, core), ka: 8 (over z).
Axes of the slice: x: 4, y: 4, z: 8, core: 2. Of those that a mesh axis runs over, the one named last changes fastest.
Arguments:
- queries: bfloat16 [16384, 1024], P('pb'), may hold values from -8 to 8
- keys: bfloat16 [8, 2048, 128], P('ka', 'pb'), may hold values from -4 to 4
- values: bfloat16 [8, 2048, 128], P('ka', 'pb'), may hold values from -4 to 4
- span_of: int32 [64], replicated, may hold values from 0 to 63, as said below
Outputs:
- attended: bfloat16 [16384, 1024], P('pb', 'ka')
- log_norm: float32 [8, 16384], P('ka', 'pb')
The draws below stay inside these ranges and needn't reach their ends.
Inputs may be any that keep to these rules, and one draw needn't show every extreme that they name: `span_of`: for each index p of pb, slots 2 p and 2 p + 1 hold a span c and its mirror 64 - 1 - c, in either order; every span is held once.
All inputs are finite; a program needn't handle non-finite values.
Results may differ from the reference program's by a relative error of at most 0.018.
Values may be sent and summed in bfloat16 or wider, within the bound.
No kernel may reach another device: no remote copies, remote signals or barrier semaphores. Data moves between devices by JAX's collectives and lax.ppermute only.
A program may use at most 128 MiB of HBM per device.

```python
import math
import jax
import jax.numpy as jnp
from jax import lax

H = 8
DH = 128
SPAN = 256
SLOTS = 64
SEQ = 16384
GROUP_ROWS = 2048
N_KA = 8


def draw_queries(key, part):
    key = jax.random.fold_in(key, 3)
    first = jax.random.fold_in(key, 0)
    return jnp.clip(jax.random.normal(first, (SEQ, H * DH), jnp.float32), -4.0, 4.0).astype(jnp.bfloat16)


def draw_keys(key, part):
    key = jax.random.fold_in(key, 5)
    first = jax.random.fold_in(key, 0)
    return jnp.clip(jax.random.normal(first, (N_KA, GROUP_ROWS, DH), jnp.float32), -4.0, 4.0).astype(jnp.bfloat16)


def draw_span_of(key, part):
    key = jax.random.fold_in(key, 7)
    first, second = jax.random.split(key, 2)
    half = SLOTS // 2
    order = jax.random.permutation(first, half).astype(jnp.int32)
    flip = jax.random.randint(second, (half,), 0, 2)
    mirror = SLOTS - 1 - order
    lower = jnp.where(flip == 1, mirror, order)
    upper = jnp.where(flip == 1, order, mirror)
    return jnp.stack([lower, upper], axis=1).reshape(SLOTS).astype(jnp.int32)


def shard_levels(key, extent, pieces, least, high):
    gain = 1.0
    for dim, shards_of in pieces:
        steps = jax.random.uniform(jax.random.fold_in(jax.random.fold_in(key, 6), dim), (shards_of,), jnp.float32, least / len(pieces), high / len(pieces))
        gain = gain * jnp.repeat(jnp.exp(steps), extent[dim] // shards_of).reshape((-1,) + (1,) * (len(extent) - 1 - dim))
    return gain


def scatter_about(own_key, extent, spread, reach, cuts=(), kind=jnp.bfloat16):
    result = jax.random.normal(own_key, extent, jnp.float32) * spread
    if len(cuts) > 0:
        result = shard_levels(own_key, extent, cuts, -0.22, 0.18) * result
    return jnp.clip(result, min=-reach, max=reach).astype(kind)


def setup_inputs(seed: int = 0) -> dict:
    key_of = jax.random.split(jax.random.key(seed), 5)
    return {
        "queries": draw_queries(jax.random.fold_in(key_of[4], 71), 0),
        "keys": draw_keys(jax.random.fold_in(key_of[4], 71), 0),
        "values": scatter_about(key_of[2], (N_KA, GROUP_ROWS, DH), 1.0, 4.0, ((0, 8), (1, 32))),
        "span_of": draw_span_of(jax.random.fold_in(key_of[4], 71), 0),
    }


NEG = -1e+30

def reference(queries, keys, values, span_of):
    seq = queries.shape[0]
    width = queries.shape[1]
    head_dim = keys.shape[2]
    heads = width // head_dim
    key_rows = SPAN // N_KA
    scale = 1.0 / math.sqrt(head_dim)
    query_pos = (span_of[:, None] * SPAN + jnp.arange(SPAN, dtype=jnp.int32)[None, :]).reshape(-1).astype(jnp.int32)
    index = jnp.arange(GROUP_ROWS, dtype=jnp.int32)
    base_pos = span_of[index // key_rows] * SPAN + index % key_rows * N_KA
    key_pos = (base_pos[None, :] + jnp.arange(N_KA, dtype=jnp.int32)[:, None]).astype(jnp.int32)
    block = math.gcd(seq, 512)

    def one_block(start):
        query_block = lax.dynamic_slice_in_dim(queries, start, block, 0).astype(jnp.float32).reshape(block, heads, head_dim)
        query_block_pos = lax.dynamic_slice_in_dim(query_pos, start, block, 0)

        def one_group(group):
            group_keys = keys[group].astype(jnp.float32)
            group_values = values[group].astype(jnp.float32)
            group_pos = key_pos[group]
            scores = jnp.einsum('qhd,kd->qhk', query_block, group_keys) * scale
            seen = (group_pos[None, :] <= query_block_pos[:, None])[:, None, :]
            best = lax.optimization_barrier(jnp.max(jnp.where(seen, scores, NEG), axis=2))
            weights = jnp.where(seen, jnp.exp(scores - best[..., None]), 0.0)
            total = lax.optimization_barrier(jnp.sum(weights, axis=2))
            rounded = lax.optimization_barrier(weights.astype(jnp.bfloat16)).astype(jnp.float32)
            accum = jnp.einsum('qhk,kd->qhd', rounded, group_values)
            partial_value = (accum / jnp.maximum(total, 1.0)[..., None]).astype(jnp.bfloat16)
            return (partial_value, best, total)
        partial_value, best, total = lax.map(one_group, jnp.arange(N_KA, dtype=jnp.int32))
        partial_value = lax.optimization_barrier(partial_value).astype(jnp.float32)
        top = lax.optimization_barrier(jnp.max(best, axis=0))
        share = total * jnp.exp(best - top)
        norm = lax.optimization_barrier(jnp.sum(share, axis=0))
        merged = lax.optimization_barrier(jnp.sum(share[..., None] * partial_value, axis=0)) / norm[..., None]
        return (merged.astype(jnp.bfloat16).reshape(block, width), top + jnp.log(norm))
    starts = jnp.arange(seq // block, dtype=jnp.int32) * block
    outputs, norms = lax.map(one_block, starts)
    attended = outputs.reshape(seq, width)
    log_norm = norms.reshape(seq, heads).T
    return (attended, log_norm)
```

```python
import functools
import math

import jax
import jax.numpy as jnp
from jax import lax
from jax.experimental import pallas as pl
from jax.experimental.pallas import tpu as pltpu
from jax.sharding import PartitionSpec as P

AXES = ("pb", "ka")
NEG = -1e30
FAR = 3e30
LN2 = math.log(2.0)
PARTS = 4
ROWS = 256
HEAD = 128
LINES = 144


def pairs(move):
    out = []
    for y in range(4):
        for x in range(4):
            for c in range(2):
                for z in range(8):
                    ty, tx, tc, tz = move(y, x, c, z)
                    out.append((((y * 4 + x) * 2 + c) * 8 + z, ((ty * 4 + tx) * 2 + tc) * 8 + tz))
    return out


def flip(core, which):
    return (1, 3)[which ^ core]


def send(value, axis, which=0):
    moves = {
        "x": lambda y, x, c, z: (y, x ^ flip(c, which), c, z),
        "y": lambda y, x, c, z: (y ^ flip(c, which), x, c, z),
        "z": lambda y, x, c, z: (y, x, c, z ^ (2 * flip(c, which))),
        "core": lambda y, x, c, z: (y, x, 1 - c, z),
        "team": lambda y, x, c, z: (y, x, c, z ^ 1),
    }
    return lax.ppermute(value, AXES, pairs(moves[axis]))


def double(value, axis):
    held = jnp.concatenate([value, send(value, axis, 0)], axis=0)
    return jnp.concatenate([held, send(held, axis, 1)], axis=0)


def spread(value, axis):
    near = send(value, axis, 0)
    far = send(value, axis, 1)
    return [value, near, far, send(near, axis, 1)]


def prepare(span, place, own, other, high, low):
    pb = place[0]
    for q, ref in enumerate((own, other)):
        p = pb ^ q
        flag = (span[2 * p] >= 32).astype(jnp.int32)
        for out, slot in ((low, flag), (high, 1 - flag)):
            rows = ref[pl.ds(pl.multiple_of(slot * ROWS, ROWS), ROWS), :]
            for h in range(2):
                block = rows[:, h * HEAD : (h + 1) * HEAD].astype(jnp.float32)
                at = (q * 2 + h) * ROWS
                out[:, at : at + ROWS] = block.T.astype(jnp.bfloat16)


def absorb(part, scale, span, place, first_half, second_half, high, low, *refs):
    start = part == 0
    if start:
        olds = (None, None, None)
        acc_high, acc_low, stats, keys, values, lines = refs
    else:
        olds = refs[:3]
        acc_high, acc_low, stats, keys, values, lines = refs[3:]
    pb, z = place[0], place[1]
    core = pb % 2
    y, x = pb // 8, pb // 2 % 4
    near, far = 1 + 2 * core, 3 - 2 * core

    def lowest(p):
        s = span[2 * p]
        return jnp.minimum(s, 63 - s)

    mine = (lowest(pb), lowest(pb ^ 1))
    seen_low, seen_high = [], []
    for e in range(8):
        half, i = e // 4, e % 4
        src = (first_half, second_half)[half]
        inner = (near if i & 1 else 0) ^ (far if i & 2 else 0)
        outer = (near if part & 1 else 0) ^ (far if part & 2 else 0)
        ty, tx = (y ^ outer, x ^ inner) if half == 0 else (y ^ inner, x ^ outer)
        p = (ty * 4 + tx) * 2 + core
        flag = (span[2 * p] >= 32).astype(jnp.int32)
        s = lowest(p)
        seen_low.append([s < c for c in mine])
        seen_high.append([s > c for c in mine])
        for at, slot in ((0, flag), (512, 1 - flag)):
            for g in range(2):
                row = at + e * 64 + g * 32
                keys[row : row + 32, :] = src[i * 2 + g, 0, slot]
                values[row : row + 32, :] = src[i * 2 + g, 1, slot]
    lines[0:HEAD, :] = values[...].astype(jnp.float32).T.astype(jnp.bfloat16)
    lines[HEAD:LINES, :] = jnp.ones((LINES - HEAD, 1024), jnp.bfloat16)
    if start:
        row = lax.broadcasted_iota(jnp.int32, (64, ROWS), 0)
        column = lax.broadcasted_iota(jnp.int32, (64, ROWS), 1)
        edges = []
        for a, b in ((z, z ^ (2 * near)), (z ^ (2 * far), z ^ (2 * far) ^ (2 * near))):
            edges.append(row % 32 * 8 + jnp.where(row < 32, a, b) <= column)

    def update(which, q, at, old_acc, acc, s, free, seen):
        blocks = [s[free + 64 * e : free + 64 * e + 64] for e in range(8)]
        diagonal = start and q == 0
        if diagonal:
            for half in range(2):
                blocks[4 * half] = jnp.where(edges[half], blocks[4 * half], -FAR)
        tops = []
        for e, block in enumerate(blocks):
            best = jnp.max(block, axis=0, keepdims=True)
            if not (diagonal and e % 4 == 0):
                best = jnp.where(seen[e][q], best, NEG)
            tops.append(best)
        if free:
            tops.append(jnp.max(s[:free], axis=0, keepdims=True))
        top = functools.reduce(jnp.maximum, tops)
        old_top = jnp.full((1, ROWS), NEG, jnp.float32) if start else olds[2][2 * which : 2 * which + 1, at : at + ROWS]
        top = jnp.maximum(jnp.maximum(top, old_top), NEG)
        base = top * scale
        weights = []
        if free:
            weights.append(jnp.exp2(s[:free] * scale - base).astype(jnp.bfloat16))
        for e, block in enumerate(blocks):
            if diagonal and e % 4 == 0:
                mine_base = base
            else:
                mine_base = jnp.where(seen[e][q], base, base + FAR)
            weights.append(jnp.exp2(block * scale - mine_base).astype(jnp.bfloat16))
        weights = jnp.concatenate(weights, axis=0)
        sums = jnp.dot(lines[:, : free + 512] if free else lines[:, :512], weights, preferred_element_type=jnp.float32)
        if start:
            acc[:, at : at + ROWS] = sums[:HEAD]
            total = sums[HEAD : HEAD + 1]
        else:
            factor = jnp.exp2(old_top * scale - base)
            acc[:, at : at + ROWS] = old_acc[:, at : at + ROWS] * factor + sums[:HEAD]
            total = olds[2][2 * which + 1 : 2 * which + 2, at : at + ROWS] * factor + sums[HEAD : HEAD + 1]
        stats[2 * which : 2 * which + 1, at : at + ROWS] = top
        stats[2 * which + 1 : 2 * which + 2, at : at + ROWS] = total

    for q in range(2):
        for h in range(2):
            at = (q * 2 + h) * ROWS
            s = jnp.dot(keys[...], high[:, at : at + ROWS], preferred_element_type=jnp.float32)
            update(0, q, at, olds[0], acc_high, s, 512, seen_high)
            s = jnp.dot(keys[0:512, :], low[:, at : at + ROWS], preferred_element_type=jnp.float32)
            update(1, q, at, olds[1], acc_low, s, 0, seen_low)


def pack(out, at, values, norms):
    out[0:HEAD, at : at + ROWS] = values.astype(jnp.bfloat16)
    one = norms.astype(jnp.bfloat16)
    rest = norms - one.astype(jnp.float32)
    two = rest.astype(jnp.bfloat16)
    three = (rest - two.astype(jnp.float32)).astype(jnp.bfloat16)
    row = lax.broadcasted_iota(jnp.int32, (LINES - HEAD, ROWS), 0)
    tail = jnp.where(row == 0, one.astype(jnp.float32), 0.0)
    tail = jnp.where(row == 1, two.astype(jnp.float32), tail)
    tail = jnp.where(row == 2, three.astype(jnp.float32), tail)
    out[HEAD:LINES, at : at + ROWS] = tail.astype(jnp.bfloat16)


def unpack(ref, at):
    tail = ref[HEAD:LINES, at : at + ROWS].astype(jnp.float32)
    return ref[0:HEAD, at : at + ROWS].astype(jnp.float32), tail[0:1] + tail[1:2] + tail[2:3]


def finish(scale, acc_high, acc_low, stats, own, own_norm, out):
    for part, acc in enumerate((acc_high, acc_low)):
        for q in range(2):
            for h in range(2):
                at = (q * 2 + h) * ROWS
                to = (part * 2 + h) * ROWS
                top = stats[2 * part : 2 * part + 1, at : at + ROWS]
                total = stats[2 * part + 1 : 2 * part + 2, at : at + ROWS]
                some = total > 0
                total = jnp.where(some, total, 1.0)
                value = acc[:, at : at + ROWS] / total
                norm = jnp.where(some, top * (scale * LN2) + jnp.log(total), NEG)
                if q == 0:
                    own[:, to : to + ROWS] = value
                    own_norm[0:1, to : to + ROWS] = norm
                else:
                    pack(out, to, value, norm)


def merge(value_a, norm_a, value_b, norm_b):
    top = jnp.maximum(norm_a, norm_b)
    a, b = jnp.exp(norm_a - top), jnp.exp(norm_b - top)
    total = a + b
    return (a * value_a + b * value_b) / total, top + jnp.log(total)


def join(place, own, own_norm, received, mine, mine_norm, out):
    head = place[1] % 2
    for part in range(2):
        for h in range(2):
            at = (part * 2 + h) * ROWS
            value, norm = unpack(received, at)
            value, norm = merge(own[:, at : at + ROWS], own_norm[0:1, at : at + ROWS], value, norm)

            @pl.when(head == h)
            def _():
                mine[:, part * ROWS : (part + 1) * ROWS] = value
                mine_norm[0:1, part * ROWS : (part + 1) * ROWS] = norm

            @pl.when(head != h)
            def _():
                pack(out, part * ROWS, value, norm)


def close(span, place, mine, mine_norm, received, attended, log_norm):
    flag = (span[2 * place[0]] >= 32).astype(jnp.int32)
    for part in range(2):
        at = part * ROWS
        value, norm = unpack(received, at)
        value, norm = merge(mine[:, at : at + ROWS], mine_norm[0:1, at : at + ROWS], value, norm)
        slot = 1 - flag if part == 0 else flag
        to = pl.ds(pl.multiple_of(slot * ROWS, ROWS), ROWS)
        attended[to, :] = value.T.astype(jnp.bfloat16)
        log_norm[:, to] = norm


def call(body, outs, n_scalars, n_arrays, scratch=(), aliases=None, flops=0, moved=0, exps=0):
    return pl.pallas_call(
        body,
        out_shape=outs,
        in_specs=[pl.BlockSpec(memory_space=pltpu.SMEM)] * n_scalars
        + [pl.BlockSpec(memory_space=pltpu.VMEM)] * n_arrays,
        out_specs=jax.tree.map(lambda _: pl.BlockSpec(memory_space=pltpu.VMEM), outs),
        scratch_shapes=list(scratch),
        input_output_aliases=aliases or {},
        compiler_params=pltpu.CompilerParams(vmem_limit_bytes=40 * 2**20),
        cost_estimate=pl.CostEstimate(flops=flops, bytes_accessed=moved, transcendentals=exps),
    )


def shape(*dims, dtype=jnp.float32):
    return jax.ShapeDtypeStruct(dims, dtype)


def local(queries, keys, values, span_of):
    bf16 = jnp.bfloat16
    pb, z = lax.axis_index("pb"), lax.axis_index("ka")
    place = jnp.stack([pb, z]).astype(jnp.int32)
    scale = 1.0 / (math.sqrt(HEAD) * LN2)

    block = jnp.stack([keys[0], values[0]]).reshape(1, 2, 2, 32, HEAD)
    held = jnp.concatenate([block, send(block, "z", 0)], axis=0)
    first = spread(double(held, "x"), "y")
    second = spread(double(send(held, "z", 1), "y"), "x")

    own = lax.dynamic_slice_in_dim(queries, z // 2 * 2 * HEAD, 2 * HEAD, 1)
    other = send(own, "core")
    wide = 4 * ROWS
    high, low = call(prepare, [shape(HEAD, wide, dtype=bf16)] * 2, 2, 2, moved=2**20)(span_of, place, own, other)

    state_shape = [shape(HEAD, wide), shape(HEAD, wide), shape(8, wide)]
    state = []
    for part in range(PARTS):
        state = call(
            functools.partial(absorb, part, scale),
            state_shape,
            2,
            4 + len(state),
            scratch=[
                pltpu.VMEM((1024, HEAD), bf16),
                pltpu.VMEM((1024, HEAD), bf16),
                pltpu.VMEM((LINES, 1024), bf16),
            ],
            aliases={6 + i: i for i in range(len(state))},
            flops=4 * 1024 * 1536 * HEAD,
            moved=3 * 2**20,
            exps=1024 * 1536,
        )(span_of, place, first[part], second[part], high, low, *state)

    own_part, own_norm, message = call(
        functools.partial(finish, scale),
        [shape(HEAD, wide), shape(8, wide), shape(LINES, wide, dtype=bf16)],
        0,
        3,
        moved=2**20,
    )(*state)
    received = send(message, "core")
    half = 2 * ROWS
    mine, mine_norm, message = call(
        join, [shape(HEAD, half), shape(8, half), shape(LINES, half, dtype=bf16)], 1, 3, moved=2**20
    )(place, own_part, own_norm, received)
    received = send(message, "team")
    return tuple(
        call(close, [shape(half, HEAD, dtype=bf16), shape(1, half)], 2, 3, moved=2**20)(
            span_of, place, mine, mine_norm, received
        )
    )


def solution(mesh):
    placed = (P("pb", None), P("ka", "pb", None), P("ka", "pb", None), P())
    return jax.shard_map(
        local, mesh=mesh, in_specs=placed, out_specs=(P("pb", "ka"), P("ka", "pb")), check_vma=False
    )
```

```python
import functools
import math

import jax
import jax.numpy as jnp
from jax import lax
from jax.experimental import pallas as pl
from jax.experimental.pallas import tpu as pltpu
from jax.sharding import PartitionSpec as P

AXES = ("pb", "ka")
NEG = -1e29
FAR = 3e30
STEPS = (0, 1, 3, 2)
ROWS = 256
HEAD = 128
BF16 = jnp.bfloat16
F32 = jnp.float32
SCALE = 1.0 / (math.sqrt(HEAD) * math.log(2.0))


def send(value, move):
    pairs = []
    for y in range(4):
        for x in range(4):
            for c in range(2):
                for z in range(8):
                    ty, tx, tc, tz = move(y, x, c, z)
                    pairs.append((((y * 4 + x) * 2 + c) * 8 + z, ((ty * 4 + tx) * 2 + tc) * 8 + tz))
    return lax.ppermute(value, AXES, pairs)


def along_z(step):
    return lambda y, x, c, z: (y, x, c, z ^ (2 * step))


def along_first(step):
    return lambda y, x, c, z: (y, x ^ step, c, z) if c == 0 else (y ^ step, x, c, z)


def along_second(step):
    return lambda y, x, c, z: (y ^ step, x, c, z) if c == 0 else (y, x ^ step, c, z)


def spread(value, along):
    return [value] + [send(value, along(step)) for step in STEPS[1:]]


def partner(c, z):
    return z ^ 1 if c == 0 else (z + 8 + (1 if z % 2 else -1)) % 8


def lowest(span, p):
    s = span[2 * p]
    return jnp.minimum(s, 63 - s)


def pieces(norms):
    one = norms.astype(BF16).astype(F32)
    two = (norms - one).astype(BF16).astype(F32)
    return one, two, norms - one - two


def eye():
    return lax.broadcasted_iota(jnp.int32, (HEAD, HEAD), 0) == lax.broadcasted_iota(jnp.int32, (HEAD, HEAD), 1)


def to_lanes(wide):
    mask = eye()
    n = wide.shape[0] // HEAD
    return [jnp.sum(jnp.where(mask, wide[i * HEAD : (i + 1) * HEAD], 0.0), axis=0, keepdims=True) for i in range(n)]


def pack(out, at, norms):
    terms = [t for row in to_lanes(norms) for t in pieces(row)]
    room = out.shape[0] - at
    rows = jnp.concatenate(terms + [jnp.zeros((room - len(terms), HEAD), F32)], axis=0)
    out[at:, :] = rows.astype(BF16)


def unpack(ref, at, block):
    terms = ref[at:, :].astype(F32)
    mask = eye()
    parts = [jnp.where(mask, terms[3 * block + i : 3 * block + i + 1], 0.0).astype(BF16) for i in range(3)]
    return jnp.dot(jnp.concatenate(parts, axis=1), jnp.ones((3 * HEAD, HEAD), BF16), preferred_element_type=F32)


def prepare(span, place, own, other, both, flags, tables):
    pb, z = place[0], place[1]
    core = pb % 2
    y, x = pb // 8, pb // 2 % 4
    mine = (lowest(span, pb), lowest(span, pb ^ 1))
    for q, ref in enumerate((own, other)):
        flag = (span[2 * (pb ^ q)] >= 32).astype(jnp.int32)
        for half, slot in ((0, flag), (1, 1 - flag)):
            rows = ref[pl.ds(pl.multiple_of(slot * ROWS, ROWS), ROWS), :]
            for h in range(2):
                both[q, h * ROWS : (h + 1) * ROWS, half * HEAD : (half + 1) * HEAD] = rows[:, h * HEAD : (h + 1) * HEAD]
    for part in range(4):
        for i in range(4):
            ty = jnp.where(core == 0, y ^ STEPS[part], y ^ STEPS[i])
            tx = jnp.where(core == 0, x ^ STEPS[i], x ^ STEPS[part])
            p = (ty * 4 + tx) * 2 + core
            flags[part, i] = jnp.full((16, HEAD), jnp.where(span[2 * p] >= 32, 1.0, 0.0), F32).astype(BF16)
            for q in range(2):
                value = jnp.where(lowest(span, p) < mine[q], 1.0, 0.0)
                if part == 0 and q == 0 and i == 0:
                    value = jnp.float32(1.0)
                flags[part, 4 + 4 * q + i] = jnp.full((16, HEAD), value, F32).astype(BF16)
                tables[part, 4 * q + i] = jnp.full((8, HEAD), value, F32)
    lane = lax.broadcasted_iota(jnp.int32, (8, HEAD), 1)
    group = z ^ (2 * jnp.where(lane < 64, jnp.where(lane < 32, 0, STEPS[1]), jnp.where(lane < 96, STEPS[2], STEPS[3])))
    tables[0, 8] = (lane % 32 * 8 + group).astype(F32)
    tables[0, 9] = jnp.full((8, HEAD), jnp.where(span[2 * pb] >= 32, 1.0, 0.0), F32)


def spread_rows(tile, n):
    return jnp.broadcast_to(tile[None], (n // 8, 8, HEAD)).reshape(n, HEAD)


def absorb(chips, which, n_blocks, *refs):
    start, last = chips[0][2] == 0, chips[0][2] == 3
    blocks, (both, flags, tables), refs = refs[:n_blocks], refs[n_blocks : n_blocks + 3], refs[n_blocks + 3 :]
    n_chips = len(chips)
    n_old = 0 if start else 3 * len(which)
    olds = [refs[3 * j : 3 * j + 3] for j in range(n_old // 3)]
    refs = refs[n_old:]
    rows = 2 * ROWS
    low_keys, low_values, keys, values = refs[-4:]
    outs = refs[:-4]

    def times(data, tile):
        return (data.reshape(HEAD // 16, 16, HEAD) * tile[None]).reshape(HEAD, HEAD)

    low_values[:, HEAD:] = jnp.ones((n_chips * HEAD, HEAD), BF16)
    kinds, tiles = [], []
    for j, q in enumerate(which):
        kinds.append([tables[part, 4 * q + i] for _, _, part, i in chips])
        if start and q == 0:
            kinds[j].append(jnp.zeros((8, HEAD), F32))
        tiles.append(len(kinds[j]))
    for at, (which_block, place, part, i) in enumerate(chips):
        to = slice(at * HEAD, (at + 1) * HEAD)
        flag = flags[part, i]
        block = blocks[which_block]
        for kv, low_ref, fold_ref in ((0, low_keys, keys), (1, low_values, values)):
            first = block[4 * place : 4 * place + 4, kv, 0].reshape(HEAD, HEAD)
            second = block[4 * place : 4 * place + 4, kv, 1].reshape(HEAD, HEAD)
            low = times(first, 1 - flag) + times(second, flag)
            high = times(first, flag) + times(second, 1 - flag)
            low_ref[to, 0:HEAD] = low
            for j, q in enumerate(which):
                kind = flags[part, 4 + 4 * q + i]
                fold_ref[j, to, 0:HEAD] = times(low, kind)
                fold_ref[j, to, HEAD:] = times(high, 1 - kind)
                if tiles[j] == 5 and i == 0:
                    fold_ref[j, 4 * HEAD :, 0:HEAD] = jnp.zeros((HEAD, HEAD), BF16)
                    fold_ref[j, 4 * HEAD :, HEAD:] = high

    contract = (((1,), (1,)), ((), ()))
    scores = []
    for j, q in enumerate(which):
        free = lax.dot_general(both[q, :, HEAD:], low_keys[...], contract, preferred_element_type=F32)
        fold = lax.dot_general(both[q], keys[j, : tiles[j] * HEAD, :], contract, preferred_element_type=F32)
        tile = [fold[:, i * HEAD : (i + 1) * HEAD] for i in range(tiles[j])]
        if tiles[j] == 5:
            row = lax.broadcasted_iota(jnp.int32, (rows, HEAD), 0) % ROWS
            edge = spread_rows(tables[0, 8], rows) <= row.astype(F32)
            tile[0] = jnp.where(edge, tile[0], -FAR)
            tile[4] = jnp.where(edge, tile[4], -FAR)
        scores.append(([free[:, i * HEAD : (i + 1) * HEAD] for i in range(n_chips)], tile))
    for j, q in enumerate(which):
        free, tile = scores[j]
        kind = kinds[j]
        bests = (
            [t + spread_rows((k - 1.0) * FAR, rows) for t, k in zip(tile, kind)],
            [t - spread_rows(k * FAR, rows) for t, k in zip(tile, kind)] + free,
        )
        bases, factors = [], []
        for k in range(2):
            at = slice(k * rows, (k + 1) * rows)
            top = jnp.max(functools.reduce(jnp.maximum, bests[k]), axis=1, keepdims=True) * SCALE
            if start:
                top = jnp.broadcast_to(jnp.maximum(top, NEG), (rows, HEAD))
            else:
                old = olds[j][1][at, :]
                top = jnp.maximum(top, old)
                factors.append(jnp.exp2(old - top))
            bases.append(top)
        low_sum = jnp.zeros((rows, HEAD), F32)
        high_sum = jnp.zeros((rows, HEAD), F32)
        weights = []
        for t, k in zip(tile, kind):
            base = jnp.where(spread_rows(k, rows) > 0, bases[0], bases[1])
            w = jnp.exp2(t * SCALE - base)
            low_sum = low_sum + w * spread_rows(k, rows)
            high_sum = high_sum + w * spread_rows(1.0 - k, rows)
            weights.append(w.astype(BF16))
        fold = jnp.dot(
            jnp.concatenate(weights, axis=1), values[j, : tiles[j] * HEAD, :], preferred_element_type=F32
        )
        weights = [jnp.exp2(t * SCALE - bases[1]).astype(BF16) for t in free]
        free = jnp.dot(jnp.concatenate(weights, axis=1), low_values[...], preferred_element_type=F32)
        parts = (fold[:, :HEAD], fold[:, HEAD:] + free[:, :HEAD])
        totals = (
            jnp.broadcast_to(jnp.sum(low_sum, axis=1, keepdims=True), (rows, HEAD)),
            jnp.sum(high_sum, axis=1, keepdims=True) + free[:, HEAD:],
        )
        norms = []
        for k in range(2):
            at = slice(k * rows, (k + 1) * rows)
            value, total = parts[k], totals[k]
            if not start:
                value = olds[j][0][at, :] * factors[k] + value
                total = olds[j][2][at, :] * factors[k] + total
            if last and q == 1:
                some = total > 0
                total = jnp.where(some, total, 1.0)
                outs[0][at, :] = (value / total).astype(BF16)
                norms.append(jnp.where(some, bases[k] + jnp.log2(total), NEG))
            else:
                outs[3 * j][at, :] = value
                outs[3 * j + 1][at, :] = bases[k]
                outs[3 * j + 2][at, :] = total
        if last and q == 1:
            pack(outs[0], 2 * rows, jnp.concatenate(norms, axis=0))


def merge(value, top, total, other, norm):
    best = jnp.maximum(top, norm)
    a, b = jnp.exp2(top - best), jnp.exp2(norm - best)
    return value * a + other * b, best, total * a + b


def join(head, acc, tops, sums, received, *outs):
    norms = []
    for kind in range(2):
        for j in range(2):
            block = kind * 4 + head * 2 + j
            rows = slice(block * HEAD, (block + 1) * HEAD)
            to = slice((kind * 2 + j) * HEAD, (kind * 2 + j + 1) * HEAD)
            norm = unpack(received, 4 * ROWS, block)
            value, top, total = merge(acc[rows, :], tops[rows, :], sums[rows, :], received[rows, :].astype(F32), norm)
            if head == 0:
                outs[0][to, :], outs[1][to, :], outs[2][to, :] = value, top, total
            else:
                some = total > 0
                total = jnp.where(some, total, 1.0)
                outs[0][to, :] = (value / total).astype(BF16)
                norms.append(jnp.where(some, top + jnp.log2(total), NEG))
    if head == 1:
        pack(outs[0], 2 * ROWS, jnp.concatenate(norms, axis=0))


def close(tables, mine, mine_tops, mine_sums, received, attended, log_norm):
    flag = tables[0, 9]
    values, norms = [], []
    for block in range(4):
        rows = slice(block * HEAD, (block + 1) * HEAD)
        value, top, total = merge(
            mine[rows, :],
            mine_tops[rows, :],
            mine_sums[rows, :],
            received[rows, :].astype(F32),
            unpack(received, 2 * ROWS, block),
        )
        values.append(value / total)
        norms += to_lanes((top + jnp.log2(total)) * math.log(2.0))
    for slot in range(2):
        for j in range(2):
            low, high = values[j], values[2 + j]
            swap = spread_rows(flag, HEAD) > 0
            pair = (high, low) if slot == 0 else (low, high)
            rows = slice((slot * 2 + j) * HEAD, (slot * 2 + j + 1) * HEAD)
            attended[rows, :] = jnp.where(swap, *pair).astype(BF16)
            pair = (norms[2 + j], norms[j]) if slot == 0 else (norms[j], norms[2 + j])
            log_norm[:, rows] = jnp.where(flag[0:1] > 0, *pair)


def call(body, outs, *args, scalars=0, scratch=(), aliases=None, flops=0, moved=2**20, exps=0):
    return pl.pallas_call(
        body,
        out_shape=outs,
        in_specs=[pl.BlockSpec(memory_space=pltpu.SMEM if i < scalars else pltpu.VMEM) for i in range(len(args))],
        out_specs=jax.tree.map(lambda _: pl.BlockSpec(memory_space=pltpu.VMEM), outs),
        scratch_shapes=list(scratch),
        input_output_aliases=aliases or {},
        compiler_params=pltpu.CompilerParams(vmem_limit_bytes=40 * 2**20),
        cost_estimate=pl.CostEstimate(flops=flops, bytes_accessed=moved, transcendentals=exps),
    )(*args)


def shape(*dims, dtype=F32):
    return jax.ShapeDtypeStruct(dims, dtype)


def attend(chips, which, blocks, ready, state):
    n, n_chips = len(which), len(chips)
    start = chips[0][2] == 0
    message = chips[0][2] == 3 and which == (1,)
    outs = [shape(4 * ROWS + 32, HEAD, dtype=BF16)] if message else [shape(4 * ROWS, HEAD)] * (3 * n)
    wide = n_chips + 1 if start else n_chips
    return call(
        functools.partial(absorb, chips, which, len(blocks)),
        outs,
        *blocks,
        *ready,
        *state,
        scratch=[
            pltpu.VMEM((n_chips * HEAD, HEAD), BF16),
            pltpu.VMEM((n_chips * HEAD, 2 * HEAD), BF16),
            pltpu.VMEM((n, wide * HEAD, 2 * HEAD), BF16),
            pltpu.VMEM((n, wide * HEAD, 2 * HEAD), BF16),
        ],
        aliases={} if start or message else {len(blocks) + 3 + i: i for i in range(3 * n)},
        flops=n * n_chips * 1024 * 1024 * HEAD,
        moved=n * 2 * 2**20,
        exps=n * n_chips * 128 * 1024,
    )


def get_ready(span_of, place, own, other):
    return call(
        prepare,
        [shape(2, 2 * ROWS, 2 * HEAD, dtype=BF16), shape(4, 12, 16, HEAD, dtype=BF16), shape(4, 10, 8, HEAD)],
        span_of,
        place,
        own,
        other,
        scalars=2,
    )


def swap_cores(y, x, c, z):
    return (y, x, 1 - c, z)


def local(queries, keys, values, span_of):
    pb, z = lax.axis_index("pb"), lax.axis_index("ka")
    place = jnp.stack([pb, z]).astype(jnp.int32)

    block = jnp.stack([keys[0], values[0]]).reshape(1, 2, 2, 32, HEAD)
    held = spread(block, along_z)
    held[1], queries = lax.optimization_barrier((held[1], queries))
    shared = jnp.where(pb % 2 == 0, z ^ 1, (z + 7 + 2 * (z % 2)) % 8)
    own = jnp.concatenate([lax.dynamic_slice_in_dim(queries, h * HEAD, HEAD, 1) for h in (z, shared)], axis=1)
    other = send(own, swap_cores)
    ready = get_ready(span_of, place, own, other)
    rows = spread(jnp.concatenate(held, axis=0), along_first)
    rows = [jnp.concatenate(rows[:2], axis=0), jnp.concatenate(rows[2:], axis=0)]
    *rows, both, flags, tables = lax.optimization_barrier((*rows, *ready))
    ready = (both, flags, tables)

    near = [send(half, along_second(STEPS[1])) for half in rows]
    far = [send(half, along_second(STEPS[2])) for half in rows]
    state = attend([(i // 2, i % 2, 0, i) for i in range(4)], (0, 1), rows, ready, ())
    near[0], far[1], *state = lax.optimization_barrier((near[0], far[1], *state))
    across = [send(near[0], along_second(STEPS[2])), send(far[1], along_second(STEPS[1]))]
    first = [(0, 0, 1, 0), (0, 1, 1, 1), (1, 0, 2, 2), (1, 1, 2, 3)]
    state = attend(first, (0, 1), [near[0], far[1]], ready, state)
    second = [(0, 0, 1, 2), (0, 1, 1, 3), (1, 0, 2, 0), (1, 1, 2, 1)]
    state = attend(second, (0, 1), [near[1], far[0]], ready, state)
    last = [(i // 2, i % 2, 3, i) for i in range(4)]
    (message,) = attend(last, (1,), across, ready, state[3:])
    received = send(message, swap_cores)
    state = attend(last, (0,), across, ready, state[:3])
    half = 2 * ROWS
    (message,) = call(
        functools.partial(join, 1), [shape(half + 16, HEAD, dtype=BF16)], *state, received
    )
    mine = call(functools.partial(join, 0), [shape(half, HEAD)] * 3, *state, received)
    received = send(message, lambda y, x, c, z: (y, x, c, partner(c, z)))
    return tuple(call(close, [shape(half, HEAD, dtype=BF16), shape(1, half)], ready[2], *mine, received))


def solution(mesh):
    placed = (P("pb", None), P("ka", "pb", None), P("ka", "pb", None), P())
    return jax.shard_map(
        local, mesh=mesh, in_specs=placed, out_specs=(P("pb", "ka"), P("ka", "pb")), check_vma=False
    )
```

```python
import functools
import math

import jax
import jax.numpy as jnp
from jax import lax
from jax.experimental import pallas as pl
from jax.experimental.pallas import tpu as pltpu
from jax.sharding import PartitionSpec as P

AXES = ("pb", "ka")
NEG = -1e29
FAR = 3e30
STEPS = (0, 1, 3, 2)
ROWS = 256
HEAD = 128
BF16 = jnp.bfloat16
F32 = jnp.float32
SCALE = 1.0 / (math.sqrt(HEAD) * math.log(2.0))


def send(value, move):
    pairs = []
    for y in range(4):
        for x in range(4):
            for c in range(2):
                for z in range(8):
                    ty, tx, tc, tz = move(y, x, c, z)
                    pairs.append((((y * 4 + x) * 2 + c) * 8 + z, ((ty * 4 + tx) * 2 + tc) * 8 + tz))
    return lax.ppermute(value, AXES, pairs)


def along_z(step):
    return lambda y, x, c, z: (y, x, c, z ^ (2 * step))


def along_first(step):
    return lambda y, x, c, z: (y, x ^ step, c, z) if c == 0 else (y ^ step, x, c, z)


def along_second(step):
    return lambda y, x, c, z: (y ^ step, x, c, z) if c == 0 else (y, x ^ step, c, z)


def spread(value, along):
    return [value] + [send(value, along(step)) for step in STEPS[1:]]


def partner(c, z):
    return z ^ 1 if c == 0 else (z + 8 + (1 if z % 2 else -1)) % 8


def lowest(span, p):
    s = span[2 * p]
    return jnp.minimum(s, 63 - s)


def pieces(norms):
    one = norms.astype(BF16).astype(F32)
    two = (norms - one).astype(BF16).astype(F32)
    return one, two, norms - one - two


def eye():
    return lax.broadcasted_iota(jnp.int32, (HEAD, HEAD), 0) == lax.broadcasted_iota(jnp.int32, (HEAD, HEAD), 1)


def to_lanes(wide):
    mask = eye()
    n = wide.shape[0] // HEAD
    return [jnp.sum(jnp.where(mask, wide[i * HEAD : (i + 1) * HEAD], 0.0), axis=0, keepdims=True) for i in range(n)]


def pack(out, at, norms):
    terms = [t for row in to_lanes(norms) for t in pieces(row)]
    room = out.shape[0] - at
    rows = jnp.concatenate(terms + [jnp.zeros((room - len(terms), HEAD), F32)], axis=0)
    out[at:, :] = rows.astype(BF16)


def unpack(ref, at, block):
    terms = ref[at:, :].astype(F32)
    mask = eye()
    parts = [jnp.where(mask, terms[3 * block + i : 3 * block + i + 1], 0.0).astype(BF16) for i in range(3)]
    return jnp.dot(jnp.concatenate(parts, axis=1), jnp.ones((3 * HEAD, HEAD), BF16), preferred_element_type=F32)


def tabulate(span, place, flags, tables):
    pb, z = place[0], place[1]
    core = pb % 2
    y, x = pb // 8, pb // 2 % 4
    mine = (lowest(span, pb), lowest(span, pb ^ 1))
    for part in range(4):
        for i in range(4):
            ty = jnp.where(core == 0, y ^ STEPS[part], y ^ STEPS[i])
            tx = jnp.where(core == 0, x ^ STEPS[i], x ^ STEPS[part])
            p = (ty * 4 + tx) * 2 + core
            flags[part, i] = jnp.full((16, HEAD), jnp.where(span[2 * p] >= 32, 1.0, 0.0), F32).astype(BF16)
            for q in range(2):
                value = jnp.where(lowest(span, p) < mine[q], 1.0, 0.0)
                if part == 0 and q == 0 and i == 0:
                    value = jnp.float32(1.0)
                flags[part, 4 + 4 * q + i] = jnp.full((16, HEAD), value, F32).astype(BF16)
                tables[part, 4 * q + i] = jnp.full((8, HEAD), value, F32)
    lane = lax.broadcasted_iota(jnp.int32, (8, HEAD), 1)
    group = z ^ (2 * jnp.where(lane < 64, jnp.where(lane < 32, 0, STEPS[1]), jnp.where(lane < 96, STEPS[2], STEPS[3])))
    tables[0, 8] = (lane % 32 * 8 + group).astype(F32)
    for q in range(2):
        value = jnp.full((16, HEAD), jnp.where(span[2 * (pb ^ q)] >= 32, 1.0, 0.0), F32)
        tables[0, 9 + q] = value[:8]
        flags[0, 12 + q] = value.astype(BF16)


def times(data, tile):
    n = data.shape[0]
    return (data.reshape(n // 16, 16, HEAD) * tile[None]).reshape(n, HEAD)


def arrange(flags, own, other, both):
    for q, ref in enumerate((own, other)):
        flag = flags[0, 12 + q]
        for h in range(2):
            lanes = slice(h * HEAD, (h + 1) * HEAD)
            first, second = ref[:ROWS, lanes], ref[ROWS:, lanes]
            rows = slice(h * ROWS, (h + 1) * ROWS)
            both[q, rows, :HEAD] = times(first, 1 - flag) + times(second, flag)
            both[q, rows, HEAD:] = times(first, flag) + times(second, 1 - flag)


def spread_rows(tile, n):
    return jnp.broadcast_to(tile[None], (n // 8, 8, HEAD)).reshape(n, HEAD)


def absorb(chips, which, heads, *refs):
    start, last = chips[0][2] == 0, chips[0][2] == 3
    n_blocks = 1 + max(c[0] for c in chips)
    blocks, (both, flags, tables), refs = refs[:n_blocks], refs[n_blocks : n_blocks + 3], refs[n_blocks + 3 :]
    n_old = 0 if start else 3 * len(which)
    olds = [refs[3 * j : 3 * j + 3] for j in range(n_old // 3)]
    refs = refs[n_old:]
    rows = len(heads) * ROWS
    low_keys, low_values, keys, values = refs[-4:]
    outs = refs[:-4]
    n_chips = len(chips)

    kinds, tiles = [], []
    for j, q in enumerate(which):
        kinds.append([tables[part, 4 * q + i] for _, _, part, i in chips])
        if start and q == 0:
            kinds[j].append(jnp.zeros((8, HEAD), F32))
        tiles.append(len(kinds[j]))
    first_lane = lax.broadcasted_iota(jnp.int32, (HEAD, HEAD), 1) == 0
    for at, (which_block, place, part, i) in enumerate(chips):
        to = slice(at * HEAD, (at + 1) * HEAD)
        flag = flags[part, i]
        block = blocks[which_block]
        low_values[to, HEAD:] = jnp.where(first_lane, 1.0, 0.0).astype(BF16)
        for kv, low_ref, fold_ref in ((0, low_keys, keys), (1, low_values, values)):
            first = block[4 * place : 4 * place + 4, kv, 0].reshape(HEAD, HEAD)
            second = block[4 * place : 4 * place + 4, kv, 1].reshape(HEAD, HEAD)
            low = times(first, 1 - flag) + times(second, flag)
            high = times(first, flag) + times(second, 1 - flag)
            low_ref[to, 0:HEAD] = low
            for j, q in enumerate(which):
                kind = flags[part, 4 + 4 * q + i]
                fold_ref[j, to, 0:HEAD] = times(low, kind)
                fold_ref[j, to, HEAD:] = times(high, 1 - kind)
                if tiles[j] > n_chips and at == 0:
                    fold_ref[j, n_chips * HEAD :, 0:HEAD] = jnp.zeros((HEAD, HEAD), BF16)
                    fold_ref[j, n_chips * HEAD :, HEAD:] = high

    contract = (((1,), (1,)), ((), ()))
    mine = slice(heads[0] * ROWS, heads[0] * ROWS + rows)
    for j, q in enumerate(which):
        kind = kinds[j]
        free = lax.dot_general(both[q, mine, HEAD:], low_keys[...], contract, preferred_element_type=F32)
        free = [free[:, i * HEAD : (i + 1) * HEAD] for i in range(n_chips)]
        fold = lax.dot_general(
            both[q, mine, :], keys[j, : tiles[j] * HEAD, :], contract, preferred_element_type=F32
        )
        tile = [fold[:, i * HEAD : (i + 1) * HEAD] for i in range(tiles[j])]
        if tiles[j] > n_chips:
            row = lax.broadcasted_iota(jnp.int32, (rows, HEAD), 0) % ROWS
            edge = spread_rows(tables[0, 8], rows) <= row.astype(F32)
            tile[0] = jnp.where(edge, tile[0], -FAR)
            tile[-1] = jnp.where(edge, tile[-1], -FAR)
        bests = (
            [t + spread_rows((k - 1.0) * FAR, rows) for t, k in zip(tile, kind)],
            [t - spread_rows(k * FAR, rows) for t, k in zip(tile, kind)] + free,
        )
        bases, factors = [], []
        for k in range(2):
            at = slice(k * 2 * ROWS + mine.start, k * 2 * ROWS + mine.stop)
            top = jnp.max(functools.reduce(jnp.maximum, bests[k]), axis=1, keepdims=True) * SCALE
            if start:
                top = jnp.broadcast_to(jnp.maximum(top, NEG), (rows, HEAD))
            else:
                old = olds[j][1][at, :]
                top = jnp.maximum(top, old)
                factors.append(jnp.exp2(old - top))
            bases.append(top)
        low_sum = jnp.zeros((rows, HEAD), F32)
        high_sum = jnp.zeros((rows, HEAD), F32)
        weights = []
        for t, k in zip(tile, kind):
            base = jnp.where(spread_rows(k, rows) > 0, bases[0], bases[1])
            w = jnp.exp2(t * SCALE - base)
            low_sum = low_sum + w * spread_rows(k, rows)
            high_sum = high_sum + w * spread_rows(1.0 - k, rows)
            weights.append(w.astype(BF16))
        fold = jnp.dot(
            jnp.concatenate(weights, axis=1), values[j, : tiles[j] * HEAD, :], preferred_element_type=F32
        )
        weights = [jnp.exp2(t * SCALE - bases[1]).astype(BF16) for t in free]
        free = jnp.dot(jnp.concatenate(weights, axis=1), low_values[...], preferred_element_type=F32)
        parts = (fold[:, :HEAD], fold[:, HEAD:] + free[:, :HEAD])
        totals = (low_sum, high_sum + free[:, HEAD:])
        norms = []
        for k in range(2):
            at = slice(k * 2 * ROWS + mine.start, k * 2 * ROWS + mine.stop)
            to = slice(k * rows, (k + 1) * rows)
            value, total = parts[k], totals[k]
            if not start:
                value = olds[j][0][at, :] * factors[k] + value
                total = olds[j][2][at, :] * factors[k] + total
            if last:
                total = jnp.broadcast_to(jnp.sum(total, axis=1, keepdims=True), (rows, HEAD))
            if len(outs) == 1:
                some = total > 0
                total = jnp.where(some, total, 1.0)
                outs[0][to, :] = (value / total).astype(BF16)
                norms.append(jnp.where(some, bases[k] + jnp.log2(total), NEG))
            else:
                outs[3 * j][to, :] = value
                outs[3 * j + 1][to, :] = bases[k]
                outs[3 * j + 2][to, :] = total
        if len(outs) == 1:
            pack(outs[0], 2 * rows, jnp.concatenate(norms, axis=0))


def merge(value, top, total, other, norm):
    best = jnp.maximum(top, norm)
    a, b = jnp.exp2(top - best), jnp.exp2(norm - best)
    return value * a + other * b, best, total * a + b


def join(acc, tops, sums, received, *outs):
    for block in range(4):
        rows = slice(block * HEAD, (block + 1) * HEAD)
        norm = unpack(received, 2 * ROWS, block)
        state = merge(acc[rows, :], tops[rows, :], sums[rows, :], received[rows, :].astype(F32), norm)
        outs[0][rows, :], outs[1][rows, :], outs[2][rows, :] = state


def close(tables, mine, mine_tops, mine_sums, received, attended, log_norm):
    flag = tables[0, 9]
    values, norms = [], []
    for block in range(4):
        rows = slice(block * HEAD, (block + 1) * HEAD)
        value, top, total = merge(
            mine[rows, :],
            mine_tops[rows, :],
            mine_sums[rows, :],
            received[rows, :].astype(F32),
            unpack(received, 2 * ROWS, block),
        )
        values.append(value / total)
        norms += to_lanes((top + jnp.log2(total)) * math.log(2.0))
    for slot in range(2):
        for j in range(2):
            low, high = values[j], values[2 + j]
            swap = spread_rows(flag, HEAD) > 0
            pair = (high, low) if slot == 0 else (low, high)
            rows = slice((slot * 2 + j) * HEAD, (slot * 2 + j + 1) * HEAD)
            attended[rows, :] = jnp.where(swap, *pair).astype(BF16)
            pair = (norms[2 + j], norms[j]) if slot == 0 else (norms[j], norms[2 + j])
            log_norm[:, rows] = jnp.where(flag[0:1] > 0, *pair)


def call(body, outs, *args, scalars=0, scratch=(), aliases=None):
    return pl.pallas_call(
        body,
        out_shape=outs,
        in_specs=[pl.BlockSpec(memory_space=pltpu.SMEM if i < scalars else pltpu.VMEM) for i in range(len(args))],
        out_specs=jax.tree.map(lambda _: pl.BlockSpec(memory_space=pltpu.VMEM), outs),
        scratch_shapes=list(scratch),
        input_output_aliases=aliases or {},
        compiler_params=pltpu.CompilerParams(vmem_limit_bytes=40 * 2**20),
        cost_estimate=pl.CostEstimate(flops=1024, bytes_accessed=1024, transcendentals=0),
    )(*args)


def shape(*dims, dtype=F32):
    return jax.ShapeDtypeStruct(dims, dtype)


def attend(chips, which, blocks, ready, state, heads=(0, 1), message=False):
    n, n_chips = len(which), len(chips)
    rows = 2 * len(heads) * ROWS
    outs = [shape(rows + 16, HEAD, dtype=BF16)] if message else [shape(rows, HEAD)] * (3 * n)
    wide = n_chips + 1 if chips[0][2] == 0 else n_chips
    return call(
        functools.partial(absorb, chips, which, heads),
        outs,
        *blocks,
        *ready,
        *state,
        scratch=[
            pltpu.VMEM((n_chips * HEAD, HEAD), BF16),
            pltpu.VMEM((n_chips * HEAD, 2 * HEAD), BF16),
            pltpu.VMEM((n, wide * HEAD, 2 * HEAD), BF16),
            pltpu.VMEM((n, wide * HEAD, 2 * HEAD), BF16),
        ],
        aliases={len(blocks) + 3 + i: i for i in range(3 * n)} if state and len(heads) == 2 else {},
    )


def get_ready(span_of, place, own, other):
    flags, tables = call(tabulate, [shape(4, 14, 16, HEAD, dtype=BF16), shape(4, 11, 8, HEAD)], span_of, place, scalars=2)
    (both,) = call(arrange, [shape(2, 2 * ROWS, 2 * HEAD, dtype=BF16)], flags, own, other)
    return both, flags, tables


def swap_cores(y, x, c, z):
    return (y, x, 1 - c, z)


def local(queries, keys, values, span_of):
    pb, z = lax.axis_index("pb"), lax.axis_index("ka")
    place = jnp.stack([pb, z]).astype(jnp.int32)

    block = jnp.stack([keys[0], values[0]]).reshape(1, 2, 2, 32, HEAD)
    held = spread(block, along_z)
    held[1], queries = lax.optimization_barrier((held[1], queries))
    shared = jnp.where(pb % 2 == 0, z ^ 1, (z + 7 + 2 * (z % 2)) % 8)
    own = jnp.concatenate([lax.dynamic_slice_in_dim(queries, h * HEAD, HEAD, 1) for h in (z, shared)], axis=1)
    other = send(own, swap_cores)
    ready = get_ready(span_of, place, own, other)
    rows = spread(jnp.concatenate(held, axis=0), along_first)
    rows = [jnp.concatenate(rows[:2], axis=0), jnp.concatenate(rows[2:], axis=0)]
    *rows, both, flags, tables = lax.optimization_barrier((*rows, *ready))
    ready = (both, flags, tables)

    near = [send(half, along_second(STEPS[1])) for half in rows]
    far = [send(half, along_second(STEPS[2])) for half in rows]
    state = attend([(i // 2, i % 2, 0, i) for i in range(4)], (0, 1), rows, ready, ())
    near[0], far[1], *state = lax.optimization_barrier((near[0], far[1], *state))
    across = [send(near[0], along_second(STEPS[2])), send(far[1], along_second(STEPS[1]))]
    chips = [(2 * part + i // 2, i % 2, 1 + part, i) for part in range(2) for i in range(4)]
    state = attend(chips, (0, 1), near + far, ready, state)

    chips = [(i // 2, i % 2, 3, i) for i in range(4)]
    (message,) = attend(chips, (1,), across, ready, state[3:], (1,), True)
    cross = send(message, lambda y, x, c, z: (y, x, 1 - c, partner(1 - c, z)))
    (message,) = attend(chips, (0,), across, ready, state[:3], (1,), True)
    message, *state = lax.optimization_barrier((message, *state))
    side = send(message, lambda y, x, c, z: (y, x, c, partner(c, z)))
    (message,) = attend(chips, (1,), across, ready, state[3:], (0,), True)
    mate = send(message, swap_cores)
    state = attend(chips, (0,), across, ready, state[:3], (0,))
    half = 2 * ROWS
    for message in (cross, side):
        state = call(join, [shape(half, HEAD)] * 3, *state, message)
    return tuple(call(close, [shape(half, HEAD, dtype=BF16), shape(1, half)], tables, *state, mate))


def solution(mesh):
    placed = (P("pb", None), P("ka", "pb", None), P("ka", "pb", None), P())
    return jax.shard_map(
        local, mesh=mesh, in_specs=placed, out_specs=(P("pb", "ka"), P("ka", "pb")), check_vma=False
    )
```

```python
import functools
import math

import jax
import jax.numpy as jnp
from jax import lax
from jax.experimental import pallas as pl
from jax.experimental.pallas import tpu as pltpu
from jax.sharding import PartitionSpec as P

AXES = ("pb", "ka")
NEG = -1e29
FAR = 3e30
STEPS = (0, 1, 3, 2)
ROWS = 256
HEAD = 128
BF16 = jnp.bfloat16
F32 = jnp.float32
SCALE = 1.0 / (math.sqrt(HEAD) * math.log(2.0))


def send(value, move):
    pairs = []
    for y in range(4):
        for x in range(4):
            for c in range(2):
                for z in range(8):
                    ty, tx, tc, tz = move(y, x, c, z)
                    pairs.append((((y * 4 + x) * 2 + c) * 8 + z, ((ty * 4 + tx) * 2 + tc) * 8 + tz))
    return lax.ppermute(value, AXES, pairs)


def along_z(step):
    return lambda y, x, c, z: (y, x, c, z ^ (2 * step))


def along_first(step):
    return lambda y, x, c, z: (y, x ^ step, c, z) if c == 0 else (y ^ step, x, c, z)


def along_second(step):
    return lambda y, x, c, z: (y ^ step, x, c, z) if c == 0 else (y, x ^ step, c, z)


def spread(value, along):
    return [value] + [send(value, along(step)) for step in STEPS[1:]]


def partner(c, z):
    return z ^ 1 if c == 0 else (z + 8 + (1 if z % 2 else -1)) % 8


def lowest(span, p):
    s = span[2 * p]
    return jnp.minimum(s, 63 - s)


def pieces(norms):
    one = norms.astype(BF16).astype(F32)
    two = (norms - one).astype(BF16).astype(F32)
    return one, two, norms - one - two


def eye():
    return lax.broadcasted_iota(jnp.int32, (HEAD, HEAD), 0) == lax.broadcasted_iota(jnp.int32, (HEAD, HEAD), 1)


def to_lanes(wide):
    mask = eye()
    n = wide.shape[0] // HEAD
    return [jnp.sum(jnp.where(mask, wide[i * HEAD : (i + 1) * HEAD], 0.0), axis=0, keepdims=True) for i in range(n)]


def pack(out, at, norms):
    terms = [t for row in to_lanes(norms) for t in pieces(row)]
    room = out.shape[0] - at
    rows = jnp.concatenate(terms + [jnp.zeros((room - len(terms), HEAD), F32)], axis=0)
    out[at:, :] = rows.astype(BF16)


def unpack(ref, at, block):
    terms = ref[at:, :].astype(F32)
    mask = eye()
    parts = [jnp.where(mask, terms[3 * block + i : 3 * block + i + 1], 0.0).astype(BF16) for i in range(3)]
    return jnp.dot(jnp.concatenate(parts, axis=1), jnp.ones((3 * HEAD, HEAD), BF16), preferred_element_type=F32)


def tabulate(span, place, flags, tables):
    pb, z = place[0], place[1]
    core = pb % 2
    y, x = pb // 8, pb // 2 % 4
    mine = (lowest(span, pb), lowest(span, pb ^ 1))
    for part in range(4):
        for i in range(4):
            ty = jnp.where(core == 0, y ^ STEPS[part], y ^ STEPS[i])
            tx = jnp.where(core == 0, x ^ STEPS[i], x ^ STEPS[part])
            p = (ty * 4 + tx) * 2 + core
            flags[part, i] = jnp.full((16, HEAD), jnp.where(span[2 * p] >= 32, 1.0, 0.0), F32).astype(BF16)
            for q in range(2):
                value = jnp.where(lowest(span, p) < mine[q], 1.0, 0.0)
                if part == 0 and q == 0 and i == 0:
                    value = jnp.float32(1.0)
                flags[part, 4 + 4 * q + i] = jnp.full((16, HEAD), value, F32).astype(BF16)
                tables[part, 4 * q + i] = jnp.full((8, HEAD), value, F32)
    lane = lax.broadcasted_iota(jnp.int32, (8, HEAD), 1)
    group = z ^ (2 * jnp.where(lane < 64, jnp.where(lane < 32, 0, STEPS[1]), jnp.where(lane < 96, STEPS[2], STEPS[3])))
    tables[0, 8] = (lane % 32 * 8 + group).astype(F32)
    for q in range(2):
        value = jnp.full((16, HEAD), jnp.where(span[2 * (pb ^ q)] >= 32, 1.0, 0.0), F32)
        tables[0, 9 + q] = value[:8]
        flags[0, 12 + q] = value.astype(BF16)


def times(data, tile):
    n = data.shape[0]
    return (data.reshape(n // 16, 16, HEAD) * tile[None]).reshape(n, HEAD)


def arrange(flags, own, other, both):
    for q, ref in enumerate((own, other)):
        flag = flags[0, 12 + q]
        for h in range(2):
            lanes = slice(h * HEAD, (h + 1) * HEAD)
            first, second = ref[:ROWS, lanes], ref[ROWS:, lanes]
            rows = slice(h * ROWS, (h + 1) * ROWS)
            both[q, rows, :HEAD] = times(first, 1 - flag) + times(second, flag)
            both[q, rows, HEAD:] = times(first, flag) + times(second, 1 - flag)


def spread_rows(tile, n):
    return jnp.broadcast_to(tile[None], (n // 8, 8, HEAD)).reshape(n, HEAD)


def absorb(chips, which, heads, message, *refs):
    start, last = chips[0][2] == 0, chips[0][2] == 3
    n_blocks = 1 + max(c[0] for c in chips)
    blocks, (both, flags, tables), refs = refs[:n_blocks], refs[n_blocks : n_blocks + 3], refs[n_blocks + 3 :]
    n_old = 0 if start else 3 * len(which)
    olds = [refs[3 * j : 3 * j + 3] for j in range(n_old // 3)]
    refs = refs[n_old:]
    rows = len(heads) * ROWS
    low_keys, low_values, keys, values = refs[-4:]
    outs = refs[:-4]
    n_chips = len(chips)

    kinds, tiles = [], []
    for j, q in enumerate(which):
        kinds.append([tables[part, 4 * q + i] for _, _, part, i in chips])
        if start and q == 0:
            kinds[j].append(jnp.zeros((8, HEAD), F32))
        tiles.append(len(kinds[j]))
    first_lane = lax.broadcasted_iota(jnp.int32, (HEAD, HEAD), 1) == 0
    for at, (which_block, place, part, i) in enumerate(chips):
        to = slice(at * HEAD, (at + 1) * HEAD)
        flag = flags[part, i]
        block = blocks[which_block]
        low_values[to, HEAD:] = jnp.where(first_lane, 1.0, 0.0).astype(BF16)
        for kv, low_ref, fold_ref in ((0, low_keys, keys), (1, low_values, values)):
            first = block[4 * place : 4 * place + 4, kv, 0].reshape(HEAD, HEAD)
            second = block[4 * place : 4 * place + 4, kv, 1].reshape(HEAD, HEAD)
            second_low = jnp.broadcast_to(flag[None], (HEAD // 16, 16, HEAD)).reshape(HEAD, HEAD) > 0
            low = jnp.where(second_low, second, first)
            high = jnp.where(second_low, first, second)
            low_ref[to, 0:HEAD] = low
            for j, q in enumerate(which):
                kind = flags[part, 4 + 4 * q + i]
                sees = jnp.broadcast_to(kind[None], (HEAD // 16, 16, HEAD)).reshape(HEAD, HEAD) > 0
                fold_ref[j, to, 0:HEAD] = jnp.where(sees, low, jnp.zeros_like(low))
                fold_ref[j, to, HEAD:] = jnp.where(sees, jnp.zeros_like(low), high)
                if tiles[j] > n_chips and at == 0:
                    fold_ref[j, n_chips * HEAD :, 0:HEAD] = jnp.zeros((HEAD, HEAD), BF16)
                    fold_ref[j, n_chips * HEAD :, HEAD:] = high

    contract = (((1,), (1,)), ((), ()))
    units = [(j, q, h) for j, q in enumerate(which) for h in heads]
    rows = ROWS
    n_heads = len(heads)
    norms = [[] for _ in range(2 * len(which))]

    def score(j, q, h):
        mine = slice(h * ROWS, (h + 1) * ROWS)
        free = lax.dot_general(both[q, mine, HEAD:], low_keys[...], contract, preferred_element_type=F32)
        free = [free[:, i * HEAD : (i + 1) * HEAD] for i in range(n_chips)]
        fold = lax.dot_general(
            both[q, mine, :], keys[j, : tiles[j] * HEAD, :], contract, preferred_element_type=F32
        )
        tile = [fold[:, i * HEAD : (i + 1) * HEAD] for i in range(tiles[j])]
        if tiles[j] > n_chips:
            row = lax.broadcasted_iota(jnp.int32, (rows, HEAD), 0) % ROWS
            edge = spread_rows(tables[0, 8], rows) <= row.astype(F32)
            tile[0] = jnp.where(edge, tile[0], -FAR)
            tile[-1] = jnp.where(edge, tile[-1], -FAR)
        return free, tile

    def finish(j, q, h, free, tile):
        kind = kinds[j]
        mine = slice(h * ROWS, (h + 1) * ROWS)
        short = [t.astype(BF16) for t in tile]
        pens = [jnp.concatenate([(1.0 - k) * FAR, (1.0 - k) * FAR], axis=0).astype(BF16) for k in kind]
        flips = [jnp.concatenate([k * FAR, k * FAR], axis=0).astype(BF16) for k in kind]

        def lower(t, pen):
            return (t.reshape(rows // 16, 16, HEAD) - pen[None]).reshape(rows, HEAD)

        bests = (
            [lower(t, p) for t, p in zip(short, pens)],
            [lower(t, p) for t, p in zip(short, flips)] + [t.astype(BF16) for t in free],
        )
        bases, factors = [], []
        for k in range(2):
            at = slice(k * 2 * ROWS + mine.start, k * 2 * ROWS + mine.stop)
            top = jnp.max(functools.reduce(jnp.maximum, bests[k]).astype(F32), axis=1, keepdims=True) * SCALE
            if start:
                top = jnp.broadcast_to(jnp.maximum(top, NEG), (rows, HEAD))
            else:
                old = olds[j][1][at, :]
                top = jnp.maximum(top, old)
                factors.append(jnp.exp2(old - top))
            bases.append(top)
        low_sum = jnp.zeros((rows, HEAD), F32)
        high_sum = jnp.zeros((rows, HEAD), F32)
        weights = []
        for t, k in zip(tile, kind):
            base = jnp.where(spread_rows(k, rows) > 0, bases[0], bases[1])
            w = jnp.exp2(t * SCALE - base)
            low_sum = low_sum + w * spread_rows(k, rows)
            high_sum = high_sum + w
            weights.append(w.astype(BF16))
        fold = jnp.dot(
            jnp.concatenate(weights, axis=1), values[j, : tiles[j] * HEAD, :], preferred_element_type=F32
        )
        weights = [jnp.exp2(t * SCALE - bases[1]).astype(BF16) for t in free]
        free = jnp.dot(jnp.concatenate(weights, axis=1), low_values[...], preferred_element_type=F32)
        parts = (fold[:, :HEAD], fold[:, HEAD:] + free[:, :HEAD])
        totals = (low_sum, high_sum - low_sum + free[:, HEAD:])
        for k in range(2):
            at = slice(k * 2 * ROWS + mine.start, k * 2 * ROWS + mine.stop)
            place = (k * n_heads + heads.index(h)) * ROWS
            to = slice(place, place + ROWS)
            value, total = parts[k], totals[k]
            if not start:
                value = olds[j][0][at, :] * factors[k] + value
                total = olds[j][2][at, :] * factors[k] + total
            if last:
                total = jnp.broadcast_to(jnp.sum(total, axis=1, keepdims=True), (rows, HEAD))
            if message:
                some = total > 0
                total = jnp.where(some, total, 1.0)
                outs[j][to, :] = (value / total).astype(BF16)
                norms[2 * j + k].append(jnp.where(some, bases[k] + jnp.log2(total), NEG))
            else:
                outs[3 * j][to, :] = value
                outs[3 * j + 1][to, :] = bases[k]
                outs[3 * j + 2][to, :] = total

    ahead = score(*units[0])
    for n, unit in enumerate(units):
        now = ahead
        if n + 1 < len(units):
            ahead = score(*units[n + 1])
        finish(*unit, *now)
    if message:
        for j in range(len(which)):
            pack(outs[j], 2 * n_heads * ROWS, jnp.concatenate(norms[2 * j] + norms[2 * j + 1], axis=0))


def merge(value, top, total, other, norm):
    best = jnp.maximum(top, norm)
    a, b = jnp.exp2(top - best), jnp.exp2(norm - best)
    return value * a + other * b, best, total * a + b


def join(acc, tops, sums, received, *outs):
    for block in range(4):
        rows = slice(block * HEAD, (block + 1) * HEAD)
        norm = unpack(received, 2 * ROWS, block)
        state = merge(acc[rows, :], tops[rows, :], sums[rows, :], received[rows, :].astype(F32), norm)
        outs[0][rows, :], outs[1][rows, :], outs[2][rows, :] = state


def close(tables, mine, mine_tops, mine_sums, received, attended, log_norm):
    flag = tables[0, 9]
    values, norms = [], []
    for block in range(4):
        rows = slice(block * HEAD, (block + 1) * HEAD)
        value, top, total = merge(
            mine[rows, :],
            mine_tops[rows, :],
            mine_sums[rows, :],
            received[rows, :].astype(F32),
            unpack(received, 2 * ROWS, block),
        )
        values.append(value / total)
        norms += to_lanes((top + jnp.log2(total)) * math.log(2.0))
    for slot in range(2):
        for j in range(2):
            low, high = values[j], values[2 + j]
            swap = spread_rows(flag, HEAD) > 0
            pair = (high, low) if slot == 0 else (low, high)
            rows = slice((slot * 2 + j) * HEAD, (slot * 2 + j + 1) * HEAD)
            attended[rows, :] = jnp.where(swap, *pair).astype(BF16)
            pair = (norms[2 + j], norms[j]) if slot == 0 else (norms[j], norms[2 + j])
            log_norm[:, rows] = jnp.where(flag[0:1] > 0, *pair)


def call(body, outs, *args, scalars=0, scratch=(), aliases=None):
    return pl.pallas_call(
        body,
        out_shape=outs,
        in_specs=[pl.BlockSpec(memory_space=pltpu.SMEM if i < scalars else pltpu.VMEM) for i in range(len(args))],
        out_specs=jax.tree.map(lambda _: pl.BlockSpec(memory_space=pltpu.VMEM), outs),
        scratch_shapes=list(scratch),
        input_output_aliases=aliases or {},
        compiler_params=pltpu.CompilerParams(vmem_limit_bytes=40 * 2**20),
        cost_estimate=pl.CostEstimate(flops=1024, bytes_accessed=1024, transcendentals=0),
    )(*args)


def shape(*dims, dtype=F32):
    return jax.ShapeDtypeStruct(dims, dtype)


def attend(chips, which, blocks, ready, state, heads=(0, 1), message=False):
    n, n_chips = len(which), len(chips)
    rows = 2 * len(heads) * ROWS
    outs = [shape(rows + 16, HEAD, dtype=BF16)] * n if message else [shape(rows, HEAD)] * (3 * n)
    wide = n_chips + 1 if chips[0][2] == 0 else n_chips
    return call(
        functools.partial(absorb, chips, which, heads, message),
        outs,
        *blocks,
        *ready,
        *state,
        scratch=[
            pltpu.VMEM((n_chips * HEAD, HEAD), BF16),
            pltpu.VMEM((n_chips * HEAD, 2 * HEAD), BF16),
            pltpu.VMEM((n, wide * HEAD, 2 * HEAD), BF16),
            pltpu.VMEM((n, wide * HEAD, 2 * HEAD), BF16),
        ],
        aliases={len(blocks) + 3 + i: i for i in range(3 * n)} if state and len(heads) == 2 else {},
    )


def get_ready(span_of, place, own, other):
    flags, tables = call(tabulate, [shape(4, 14, 16, HEAD, dtype=BF16), shape(4, 11, 8, HEAD)], span_of, place, scalars=2)
    (both,) = call(arrange, [shape(2, 2 * ROWS, 2 * HEAD, dtype=BF16)], flags, own, other)
    return both, flags, tables


def swap_cores(y, x, c, z):
    return (y, x, 1 - c, z)


def local(queries, keys, values, span_of):
    pb, z = lax.axis_index("pb"), lax.axis_index("ka")
    place = jnp.stack([pb, z]).astype(jnp.int32)

    block = jnp.stack([keys[0], values[0]]).reshape(1, 2, 2, 32, HEAD)
    held = spread(block, along_z)
    held[1], queries = lax.optimization_barrier((held[1], queries))
    shared = jnp.where(pb % 2 == 0, z ^ 1, (z + 7 + 2 * (z % 2)) % 8)
    own = jnp.concatenate([lax.dynamic_slice_in_dim(queries, h * HEAD, HEAD, 1) for h in (z, shared)], axis=1)
    other = send(own, swap_cores)
    ready = get_ready(span_of, place, own, other)
    rows = spread(jnp.concatenate(held, axis=0), along_first)
    rows = [jnp.concatenate(rows[:2], axis=0), jnp.concatenate(rows[2:], axis=0)]
    *rows, both, flags, tables = lax.optimization_barrier((*rows, *ready))
    ready = (both, flags, tables)

    near = [send(half, along_second(STEPS[1])) for half in rows]
    far = [send(half, along_second(STEPS[2])) for half in rows]
    state = attend([(i // 2, i % 2, 0, i) for i in range(4)], (0, 1), rows, ready, ())
    near[0], far[1], *state = lax.optimization_barrier((near[0], far[1], *state))
    across = [send(near[0], along_second(STEPS[2])), send(far[1], along_second(STEPS[1]))]
    chips = [(2 * part + i // 2, i % 2, 1 + part, i) for part in range(2) for i in range(4)]
    state = attend(chips, (0, 1), near + far, ready, state)

    chips = [(i // 2, i % 2, 3, i) for i in range(4)]
    messages = attend(chips, (1, 0), across, ready, state[3:] + state[:3], (1,), True)
    cross, side, *state = lax.optimization_barrier((*messages, *state))
    cross = send(cross, lambda y, x, c, z: (y, x, 1 - c, partner(1 - c, z)))
    side = send(side, lambda y, x, c, z: (y, x, c, partner(c, z)))
    (message,) = attend(chips, (1,), across, ready, state[3:], (0,), True)
    mate = send(message, swap_cores)
    state = attend(chips, (0,), across, ready, state[:3], (0,))
    half = 2 * ROWS
    for message in (cross, side):
        state = call(join, [shape(half, HEAD)] * 3, *state, message)
    return tuple(call(close, [shape(half, HEAD, dtype=BF16), shape(1, half)], tables, *state, mate))


def solution(mesh):
    placed = (P("pb", None), P("ka", "pb", None), P("ka", "pb", None), P())
    return jax.shard_map(
        local, mesh=mesh, in_specs=placed, out_specs=(P("pb", "ka"), P("ka", "pb")), check_vma=False
    )
```

```python
import functools
import math

import jax
import jax.numpy as jnp
from jax import lax
from jax.experimental import pallas as pl
from jax.experimental.pallas import tpu as pltpu
from jax.sharding import PartitionSpec as P

AXES = ("pb", "ka")
NEG = -1e29
FAR = 3e30
STEPS = (0, 1, 3, 2)
ROWS = 256
HEAD = 128
BF16 = jnp.bfloat16
F32 = jnp.float32
SCALE = 1.0 / (math.sqrt(HEAD) * math.log(2.0))


def send(value, move):
    pairs = []
    for y in range(4):
        for x in range(4):
            for c in range(2):
                for z in range(8):
                    ty, tx, tc, tz = move(y, x, c, z)
                    pairs.append((((y * 4 + x) * 2 + c) * 8 + z, ((ty * 4 + tx) * 2 + tc) * 8 + tz))
    return lax.ppermute(value, AXES, pairs)


def along_z(step):
    return lambda y, x, c, z: (y, x, c, z ^ (2 * step))


def along_first(step):
    return lambda y, x, c, z: (y, x ^ step, c, z) if c == 0 else (y ^ step, x, c, z)


def along_second(step):
    return lambda y, x, c, z: (y ^ step, x, c, z) if c == 0 else (y, x ^ step, c, z)


def spread(value, along):
    return [value] + [send(value, along(step)) for step in STEPS[1:]]


def partner(c, z):
    return z ^ 1 if c == 0 else (z + 8 + (1 if z % 2 else -1)) % 8


def lowest(span, p):
    s = span[2 * p]
    return jnp.minimum(s, 63 - s)


def pieces(norms):
    one = norms.astype(BF16).astype(F32)
    two = (norms - one).astype(BF16).astype(F32)
    return one, two, norms - one - two


def eye():
    return lax.broadcasted_iota(jnp.int32, (HEAD, HEAD), 0) == lax.broadcasted_iota(jnp.int32, (HEAD, HEAD), 1)


def to_lanes(wide):
    mask = eye()
    n = wide.shape[0] // HEAD
    return [jnp.sum(jnp.where(mask, wide[i * HEAD : (i + 1) * HEAD], 0.0), axis=0, keepdims=True) for i in range(n)]


def pack(out, at, norms):
    terms = [t for row in to_lanes(norms) for t in pieces(row)]
    room = out.shape[0] - at
    rows = jnp.concatenate(terms + [jnp.zeros((room - len(terms), HEAD), F32)], axis=0)
    out[at:, :] = rows.astype(BF16)


def unpack(ref, at, block):
    terms = ref[at:, :].astype(F32)
    mask = eye()
    parts = [jnp.where(mask, terms[3 * block + i : 3 * block + i + 1], 0.0).astype(BF16) for i in range(3)]
    return jnp.dot(jnp.concatenate(parts, axis=1), jnp.ones((3 * HEAD, HEAD), BF16), preferred_element_type=F32)


def tabulate(span, place, flags, tables):
    pb, z = place[0], place[1]
    core = pb % 2
    y, x = pb // 8, pb // 2 % 4
    mine = (lowest(span, pb), lowest(span, pb ^ 1))
    for part in range(4):
        for i in range(4):
            ty = jnp.where(core == 0, y ^ STEPS[part], y ^ STEPS[i])
            tx = jnp.where(core == 0, x ^ STEPS[i], x ^ STEPS[part])
            p = (ty * 4 + tx) * 2 + core
            flags[part, i] = jnp.full((16, HEAD), jnp.where(span[2 * p] >= 32, 1.0, 0.0), F32).astype(BF16)
            for q in range(2):
                value = jnp.where(lowest(span, p) < mine[q], 1.0, 0.0)
                if part == 0 and q == 0 and i == 0:
                    value = jnp.float32(1.0)
                flags[part, 4 + 4 * q + i] = jnp.full((16, HEAD), value, F32).astype(BF16)
                tables[part, 4 * q + i] = jnp.full((8, HEAD), value, F32)
    lane = lax.broadcasted_iota(jnp.int32, (8, HEAD), 1)
    group = z ^ (2 * jnp.where(lane < 64, jnp.where(lane < 32, 0, STEPS[1]), jnp.where(lane < 96, STEPS[2], STEPS[3])))
    tables[0, 8] = (lane % 32 * 8 + group).astype(F32)
    for q in range(2):
        value = jnp.full((16, HEAD), jnp.where(span[2 * (pb ^ q)] >= 32, 1.0, 0.0), F32)
        tables[0, 9 + q] = value[:8]
        flags[0, 12 + q] = value.astype(BF16)


def times(data, tile):
    n = data.shape[0]
    return (data.reshape(n // 16, 16, HEAD) * tile[None]).reshape(n, HEAD)


def arrange(flags, own, other, both):
    for q, ref in enumerate((own, other)):
        flag = flags[0, 12 + q]
        for h in range(2):
            lanes = slice(h * HEAD, (h + 1) * HEAD)
            first, second = ref[:ROWS, lanes], ref[ROWS:, lanes]
            rows = slice(h * ROWS, (h + 1) * ROWS)
            both[q, rows, :HEAD] = times(first, 1 - flag) + times(second, flag)
            both[q, rows, HEAD:] = times(first, flag) + times(second, 1 - flag)


def spread_rows(tile, n):
    return jnp.broadcast_to(tile[None], (n // 8, 8, HEAD)).reshape(n, HEAD)


def absorb(chips, which, heads, message, *refs):
    start, last = chips[0][2] == 0, chips[0][2] == 3
    n_blocks = 1 + max(c[0] for c in chips)
    blocks, (both, flags, tables), refs = refs[:n_blocks], refs[n_blocks : n_blocks + 3], refs[n_blocks + 3 :]
    n_old = 0 if start else 3 * len(which)
    olds = [refs[3 * j : 3 * j + 3] for j in range(n_old // 3)]
    refs = refs[n_old:]
    rows = len(heads) * ROWS
    low_keys, low_values, keys, values = refs[-4:]
    outs = refs[:-4]
    n_chips = len(chips)

    kinds, tiles = [], []
    for j, q in enumerate(which):
        kinds.append([tables[part, 4 * q + i] for _, _, part, i in chips])
        if start and q == 0:
            kinds[j].append(jnp.zeros((8, HEAD), F32))
        tiles.append(len(kinds[j]))
    first_lane = lax.broadcasted_iota(jnp.int32, (HEAD, HEAD), 1) == 0
    for at, (which_block, place, part, i) in enumerate(chips):
        to = slice(at * HEAD, (at + 1) * HEAD)
        flag = flags[part, i]
        block = blocks[which_block]
        low_values[to, HEAD:] = jnp.where(first_lane, 1.0, 0.0).astype(BF16)
        for kv, low_ref, fold_ref in ((0, low_keys, keys), (1, low_values, values)):
            first = block[4 * place : 4 * place + 4, kv, 0].reshape(HEAD, HEAD)
            second = block[4 * place : 4 * place + 4, kv, 1].reshape(HEAD, HEAD)
            second_low = jnp.broadcast_to(flag[None], (HEAD // 16, 16, HEAD)).reshape(HEAD, HEAD) > 0
            low = jnp.where(second_low, second, first)
            high = jnp.where(second_low, first, second)
            low_ref[to, 0:HEAD] = low
            for j, q in enumerate(which):
                kind = flags[part, 4 + 4 * q + i]
                sees = jnp.broadcast_to(kind[None], (HEAD // 16, 16, HEAD)).reshape(HEAD, HEAD) > 0
                fold_ref[j, to, 0:HEAD] = jnp.where(sees, low, jnp.zeros_like(low))
                fold_ref[j, to, HEAD:] = jnp.where(sees, jnp.zeros_like(low), high)
                if tiles[j] > n_chips and at == 0:
                    fold_ref[j, n_chips * HEAD :, 0:HEAD] = jnp.zeros((HEAD, HEAD), BF16)
                    fold_ref[j, n_chips * HEAD :, HEAD:] = high

    contract = (((1,), (1,)), ((), ()))
    units = [(j, q, h) for j, q in enumerate(which) for h in heads]
    rows = ROWS
    n_heads = len(heads)
    norms = [[] for _ in range(2 * len(which))]

    def score(j, q, h):
        mine = slice(h * ROWS, (h + 1) * ROWS)
        free = lax.dot_general(both[q, mine, HEAD:], low_keys[...], contract, preferred_element_type=F32)
        free = [free[:, i * HEAD : (i + 1) * HEAD] for i in range(n_chips)]
        fold = lax.dot_general(
            both[q, mine, :], keys[j, : tiles[j] * HEAD, :], contract, preferred_element_type=F32
        )
        tile = [fold[:, i * HEAD : (i + 1) * HEAD] for i in range(tiles[j])]
        if tiles[j] > n_chips:
            row = lax.broadcasted_iota(jnp.int32, (rows, HEAD), 0) % ROWS
            edge = spread_rows(tables[0, 8], rows) <= row.astype(F32)
            tile[0] = jnp.where(edge, tile[0], -FAR)
            tile[-1] = jnp.where(edge, tile[-1], -FAR)
        return free, tile

    def finish(j, q, h, free, tile):
        kind = kinds[j]
        mine = slice(h * ROWS, (h + 1) * ROWS)
        short = [t.astype(BF16) for t in tile]
        pens = [jnp.concatenate([(1.0 - k) * FAR, (1.0 - k) * FAR], axis=0).astype(BF16) for k in kind]
        flips = [jnp.concatenate([k * FAR, k * FAR], axis=0).astype(BF16) for k in kind]

        def lower(t, pen):
            return (t.reshape(rows // 16, 16, HEAD) - pen[None]).reshape(rows, HEAD)

        bests = (
            [lower(t, p) for t, p in zip(short, pens)],
            [lower(t, p) for t, p in zip(short, flips)] + [t.astype(BF16) for t in free],
        )
        bases, factors = [], []
        for k in range(2):
            at = slice(k * 2 * ROWS + mine.start, k * 2 * ROWS + mine.stop)
            top = jnp.max(functools.reduce(jnp.maximum, bests[k]).astype(F32), axis=1, keepdims=True) * SCALE
            if start:
                top = jnp.broadcast_to(jnp.maximum(top, NEG), (rows, HEAD))
            else:
                old = olds[j][1][at, :]
                top = jnp.maximum(top, old)
                factors.append(jnp.exp2(old - top))
            bases.append(top)
        low_sum = jnp.zeros((rows, HEAD), F32)
        high_sum = jnp.zeros((rows, HEAD), F32)
        weights = []
        for t, k in zip(tile, kind):
            base = jnp.where(spread_rows(k, rows) > 0, bases[0], bases[1])
            w = jnp.exp2(t * SCALE - base)
            low_sum = low_sum + w * spread_rows(k, rows)
            high_sum = high_sum + w
            weights.append(w.astype(BF16))
        fold = jnp.dot(
            jnp.concatenate(weights, axis=1), values[j, : tiles[j] * HEAD, :], preferred_element_type=F32
        )
        weights = [jnp.exp2(t * SCALE - bases[1]).astype(BF16) for t in free]
        free = jnp.dot(jnp.concatenate(weights, axis=1), low_values[...], preferred_element_type=F32)
        parts = (fold[:, :HEAD], fold[:, HEAD:] + free[:, :HEAD])
        totals = (low_sum, high_sum - low_sum + free[:, HEAD:])
        for k in range(2):
            at = slice(k * 2 * ROWS + mine.start, k * 2 * ROWS + mine.stop)
            place = (k * n_heads + heads.index(h)) * ROWS
            to = slice(place, place + ROWS)
            value, total = parts[k], totals[k]
            if not start:
                value = olds[j][0][at, :] * factors[k] + value
                total = olds[j][2][at, :] * factors[k] + total
            if last:
                total = jnp.broadcast_to(jnp.sum(total, axis=1, keepdims=True), (rows, HEAD))
            if message:
                some = total > 0
                total = jnp.where(some, total, 1.0)
                outs[j][to, :] = (value / total).astype(BF16)
                norms[2 * j + k].append(jnp.where(some, bases[k] + jnp.log2(total), NEG))
            else:
                outs[3 * j][to, :] = value
                outs[3 * j + 1][to, :] = bases[k]
                outs[3 * j + 2][to, :] = total

    ahead = score(*units[0])
    for n, unit in enumerate(units):
        now = ahead
        if n + 1 < len(units):
            ahead = score(*units[n + 1])
        finish(*unit, *now)
    if message:
        for j in range(len(which)):
            pack(outs[j], 2 * n_heads * ROWS, jnp.concatenate(norms[2 * j] + norms[2 * j + 1], axis=0))


def merge(value, top, total, other, norm):
    best = jnp.maximum(top, norm)
    a, b = jnp.exp2(top - best), jnp.exp2(norm - best)
    return value * a + other * b, best, total * a + b


def join(acc, tops, sums, one, two, *outs):
    for block in range(4):
        rows = slice(block * HEAD, (block + 1) * HEAD)
        state = acc[rows, :], tops[rows, :], sums[rows, :]
        for received in (one, two):
            state = merge(*state, received[rows, :].astype(F32), unpack(received, 2 * ROWS, block))
        outs[0][rows, :], outs[1][rows, :], outs[2][rows, :] = state


def close(tables, mine, mine_tops, mine_sums, received, attended, log_norm):
    flag = tables[0, 9]
    values, norms = [], []
    for block in range(4):
        rows = slice(block * HEAD, (block + 1) * HEAD)
        value, top, total = merge(
            mine[rows, :],
            mine_tops[rows, :],
            mine_sums[rows, :],
            received[rows, :].astype(F32),
            unpack(received, 2 * ROWS, block),
        )
        values.append(value / total)
        norms += to_lanes((top + jnp.log2(total)) * math.log(2.0))
    for slot in range(2):
        for j in range(2):
            low, high = values[j], values[2 + j]
            swap = spread_rows(flag, HEAD) > 0
            pair = (high, low) if slot == 0 else (low, high)
            rows = slice((slot * 2 + j) * HEAD, (slot * 2 + j + 1) * HEAD)
            attended[rows, :] = jnp.where(swap, *pair).astype(BF16)
            pair = (norms[2 + j], norms[j]) if slot == 0 else (norms[j], norms[2 + j])
            log_norm[:, rows] = jnp.where(flag[0:1] > 0, *pair)


def call(body, outs, *args, scalars=0, scratch=(), aliases=None):
    return pl.pallas_call(
        body,
        out_shape=outs,
        in_specs=[pl.BlockSpec(memory_space=pltpu.SMEM if i < scalars else pltpu.VMEM) for i in range(len(args))],
        out_specs=jax.tree.map(lambda _: pl.BlockSpec(memory_space=pltpu.VMEM), outs),
        scratch_shapes=list(scratch),
        input_output_aliases=aliases or {},
        compiler_params=pltpu.CompilerParams(vmem_limit_bytes=40 * 2**20),
        cost_estimate=pl.CostEstimate(flops=1024, bytes_accessed=1024, transcendentals=0),
    )(*args)


def shape(*dims, dtype=F32):
    return jax.ShapeDtypeStruct(dims, dtype)


def attend(chips, which, blocks, ready, state, heads=(0, 1), message=False):
    n, n_chips = len(which), len(chips)
    rows = 2 * len(heads) * ROWS
    outs = [shape(rows + 16, HEAD, dtype=BF16)] * n if message else [shape(rows, HEAD)] * (3 * n)
    wide = n_chips + 1 if chips[0][2] == 0 else n_chips
    return call(
        functools.partial(absorb, chips, which, heads, message),
        outs,
        *blocks,
        *ready,
        *state,
        scratch=[
            pltpu.VMEM((n_chips * HEAD, HEAD), BF16),
            pltpu.VMEM((n_chips * HEAD, 2 * HEAD), BF16),
            pltpu.VMEM((n, wide * HEAD, 2 * HEAD), BF16),
            pltpu.VMEM((n, wide * HEAD, 2 * HEAD), BF16),
        ],
        aliases={len(blocks) + 3 + i: i for i in range(3 * n)} if state and len(heads) == 2 else {},
    )


def get_ready(span_of, place, own, other):
    flags, tables = call(tabulate, [shape(4, 14, 16, HEAD, dtype=BF16), shape(4, 11, 8, HEAD)], span_of, place, scalars=2)
    (both,) = call(arrange, [shape(2, 2 * ROWS, 2 * HEAD, dtype=BF16)], flags, own, other)
    return both, flags, tables


def swap_cores(y, x, c, z):
    return (y, x, 1 - c, z)


def local(queries, keys, values, span_of):
    pb, z = lax.axis_index("pb"), lax.axis_index("ka")
    place = jnp.stack([pb, z]).astype(jnp.int32)

    block = jnp.stack([keys[0], values[0]]).reshape(1, 2, 2, 32, HEAD)
    held = spread(block, along_z)
    held[1], queries = lax.optimization_barrier((held[1], queries))
    shared = jnp.where(pb % 2 == 0, z ^ 1, (z + 7 + 2 * (z % 2)) % 8)
    own = jnp.concatenate([lax.dynamic_slice_in_dim(queries, h * HEAD, HEAD, 1) for h in (z, shared)], axis=1)
    other = send(own, swap_cores)
    ready = get_ready(span_of, place, own, other)
    rows = spread(jnp.concatenate(held, axis=0), along_first)
    rows = [jnp.concatenate(rows[:2], axis=0), jnp.concatenate(rows[2:], axis=0)]
    both, flags, tables = ready
    *rows, flags, tables = lax.optimization_barrier((*rows, flags, tables))
    ready = (both, flags, tables)

    near = [send(half, along_second(STEPS[1])) for half in rows]
    far = [send(half, along_second(STEPS[2])) for half in rows]
    state = attend([(i // 2, i % 2, 0, i) for i in range(4)], (0, 1), rows, ready, ())
    near[0], far[1], *state = lax.optimization_barrier((near[0], far[1], *state))
    across = [send(near[0], along_second(STEPS[2])), send(far[1], along_second(STEPS[1]))]
    chips = [(2 * part + i // 2, i % 2, 1 + part, i) for part in range(2) for i in range(4)]
    state = attend(chips, (0, 1), near + far, ready, state)

    chips = [(i // 2, i % 2, 3, i) for i in range(4)]
    messages = attend(chips, (1, 0), across, ready, state[3:] + state[:3], (1,), True)
    cross, side, *state = lax.optimization_barrier((*messages, *state))
    cross = send(cross, lambda y, x, c, z: (y, x, 1 - c, partner(1 - c, z)))
    side = send(side, lambda y, x, c, z: (y, x, c, partner(c, z)))
    (message,) = attend(chips, (1,), across, ready, state[3:], (0,), True)
    mate = send(message, swap_cores)
    state = attend(chips, (0,), across, ready, state[:3], (0,))
    half = 2 * ROWS
    state = call(join, [shape(half, HEAD)] * 3, *state, cross, side)
    return tuple(call(close, [shape(half, HEAD, dtype=BF16), shape(1, half)], tables, *state, mate))


def solution(mesh):
    placed = (P("pb", None), P("ka", "pb", None), P("ka", "pb", None), P())
    return jax.shard_map(
        local, mesh=mesh, in_specs=placed, out_specs=(P("pb", "ka"), P("ka", "pb")), check_vma=False
    )
```

```python
import functools
import math

import jax
import jax.numpy as jnp
from jax import lax
from jax.experimental import pallas as pl
from jax.experimental.pallas import tpu as pltpu
from jax.sharding import PartitionSpec as P

AXES = ("pb", "ka")
NEG = -1e29
FAR = 3e30
STEPS = (0, 1, 3, 2)
ROWS = 256
HEAD = 128
BF16 = jnp.bfloat16
F32 = jnp.float32
SCALE = 1.0 / (math.sqrt(HEAD) * math.log(2.0))


def send(value, move):
    pairs = []
    for y in range(4):
        for x in range(4):
            for c in range(2):
                for z in range(8):
                    ty, tx, tc, tz = move(y, x, c, z)
                    pairs.append((((y * 4 + x) * 2 + c) * 8 + z, ((ty * 4 + tx) * 2 + tc) * 8 + tz))
    return lax.ppermute(value, AXES, pairs)


def along_z(step):
    return lambda y, x, c, z: (y, x, c, z ^ (2 * step))


def along_first(step):
    return lambda y, x, c, z: (y, x ^ step, c, z) if c == 0 else (y ^ step, x, c, z)


def along_second(step):
    return lambda y, x, c, z: (y ^ step, x, c, z) if c == 0 else (y, x ^ step, c, z)


def spread(value, along):
    return [value] + [send(value, along(step)) for step in STEPS[1:]]


def partner(c, z):
    return z ^ 1 if c == 0 else (z + 8 + (1 if z % 2 else -1)) % 8


def lowest(span, p):
    s = span[2 * p]
    return jnp.minimum(s, 63 - s)


def pieces(norms):
    one = norms.astype(BF16).astype(F32)
    two = (norms - one).astype(BF16).astype(F32)
    return one, two, norms - one - two


def eye():
    return lax.broadcasted_iota(jnp.int32, (HEAD, HEAD), 0) == lax.broadcasted_iota(jnp.int32, (HEAD, HEAD), 1)


def to_lanes(wide):
    mask = eye()
    n = wide.shape[0] // HEAD
    return [jnp.sum(jnp.where(mask, wide[i * HEAD : (i + 1) * HEAD], 0.0), axis=0, keepdims=True) for i in range(n)]


def pack(out, at, norms):
    terms = [t for row in to_lanes(norms) for t in pieces(row)]
    room = out.shape[0] - at
    rows = jnp.concatenate(terms + [jnp.zeros((room - len(terms), HEAD), F32)], axis=0)
    out[at:, :] = rows.astype(BF16)


def unpack(ref, at, block):
    terms = ref[at:, :].astype(F32)
    mask = eye()
    parts = [jnp.where(mask, terms[3 * block + i : 3 * block + i + 1], 0.0).astype(BF16) for i in range(3)]
    return jnp.dot(jnp.concatenate(parts, axis=1), jnp.ones((3 * HEAD, HEAD), BF16), preferred_element_type=F32)


def tabulate(span, place, flags, tables):
    pb, z = place[0], place[1]
    core = pb % 2
    y, x = pb // 8, pb // 2 % 4
    mine = (lowest(span, pb), lowest(span, pb ^ 1))
    for part in range(4):
        for i in range(4):
            ty = jnp.where(core == 0, y ^ STEPS[part], y ^ STEPS[i])
            tx = jnp.where(core == 0, x ^ STEPS[i], x ^ STEPS[part])
            p = (ty * 4 + tx) * 2 + core
            flags[part, i] = jnp.full((16, HEAD), jnp.where(span[2 * p] >= 32, 1.0, 0.0), F32).astype(BF16)
            for q in range(2):
                value = jnp.where(lowest(span, p) < mine[q], 1.0, 0.0)
                if part == 0 and q == 0 and i == 0:
                    value = jnp.float32(1.0)
                flags[part, 4 + 4 * q + i] = jnp.full((16, HEAD), value, F32).astype(BF16)
                tables[part, 4 * q + i] = jnp.full((8, HEAD), value, F32)
    lane = lax.broadcasted_iota(jnp.int32, (8, HEAD), 1)
    group = z ^ (2 * jnp.where(lane < 64, jnp.where(lane < 32, 0, STEPS[1]), jnp.where(lane < 96, STEPS[2], STEPS[3])))
    tables[0, 8] = (lane % 32 * 8 + group).astype(F32)
    for q in range(2):
        value = jnp.full((16, HEAD), jnp.where(span[2 * (pb ^ q)] >= 32, 1.0, 0.0), F32)
        tables[0, 9 + q] = value[:8]
        flags[0, 12 + q] = value.astype(BF16)


def times(data, tile):
    n = data.shape[0]
    return (data.reshape(n // 16, 16, HEAD) * tile[None]).reshape(n, HEAD)


def arrange(flags, own, other, both):
    for q, ref in enumerate((own, other)):
        flag = flags[0, 12 + q]
        for h in range(2):
            lanes = slice(h * HEAD, (h + 1) * HEAD)
            first, second = ref[:ROWS, lanes], ref[ROWS:, lanes]
            rows = slice(h * ROWS, (h + 1) * ROWS)
            both[q, rows, :HEAD] = times(first, 1 - flag) + times(second, flag)
            both[q, rows, HEAD:] = times(first, flag) + times(second, 1 - flag)


def spread_rows(tile, n):
    return jnp.broadcast_to(tile[None], (n // 8, 8, HEAD)).reshape(n, HEAD)


def absorb(chips, which, heads, message, *refs):
    start, last = chips[0][2] == 0, chips[0][2] == 3
    n_blocks = 1 + max(c[0] for c in chips)
    blocks, (both, flags, tables), refs = refs[:n_blocks], refs[n_blocks : n_blocks + 3], refs[n_blocks + 3 :]
    n_old = 0 if start else 3 * len(which)
    olds = [refs[3 * j : 3 * j + 3] for j in range(n_old // 3)]
    refs = refs[n_old:]
    rows = len(heads) * ROWS
    low_keys, low_values, keys, values = refs[-4:]
    outs = refs[:-4]
    n_chips = len(chips)

    kinds, tiles = [], []
    for j, q in enumerate(which):
        kinds.append([tables[part, 4 * q + i] for _, _, part, i in chips])
        if start and q == 0:
            kinds[j].append(jnp.zeros((8, HEAD), F32))
        tiles.append(len(kinds[j]))
    first_lane = lax.broadcasted_iota(jnp.int32, (HEAD, HEAD), 1) == 0
    for at, (which_block, place, part, i) in enumerate(chips):
        to = slice(at * HEAD, (at + 1) * HEAD)
        flag = flags[part, i]
        block = blocks[which_block]
        low_values[to, HEAD:] = jnp.where(first_lane, 1.0, 0.0).astype(BF16)
        for kv, low_ref, fold_ref in ((0, low_keys, keys), (1, low_values, values)):
            first = block[4 * place : 4 * place + 4, kv, 0].reshape(HEAD, HEAD)
            second = block[4 * place : 4 * place + 4, kv, 1].reshape(HEAD, HEAD)
            second_low = jnp.broadcast_to(flag[None], (HEAD // 16, 16, HEAD)).reshape(HEAD, HEAD) > 0
            low = jnp.where(second_low, second, first)
            high = jnp.where(second_low, first, second)
            low_ref[to, 0:HEAD] = low
            for j, q in enumerate(which):
                kind = flags[part, 4 + 4 * q + i]
                sees = jnp.broadcast_to(kind[None], (HEAD // 16, 16, HEAD)).reshape(HEAD, HEAD) > 0
                fold_ref[j, to, 0:HEAD] = jnp.where(sees, low, jnp.zeros_like(low))
                fold_ref[j, to, HEAD:] = jnp.where(sees, jnp.zeros_like(low), high)
                if tiles[j] > n_chips and at == 0:
                    fold_ref[j, n_chips * HEAD :, 0:HEAD] = jnp.zeros((HEAD, HEAD), BF16)
                    fold_ref[j, n_chips * HEAD :, HEAD:] = high

    contract = (((1,), (1,)), ((), ()))
    units = [(j, q, h) for j, q in enumerate(which) for h in heads]
    rows = ROWS
    n_heads = len(heads)
    norms = [[] for _ in range(2 * len(which))]

    def score(j, q, h):
        mine = slice(h * ROWS, (h + 1) * ROWS)
        free = lax.dot_general(both[q, mine, HEAD:], low_keys[...], contract, preferred_element_type=F32)
        free = [free[:, i * HEAD : (i + 1) * HEAD] for i in range(n_chips)]
        fold = lax.dot_general(
            both[q, mine, :], keys[j, : tiles[j] * HEAD, :], contract, preferred_element_type=F32
        )
        tile = [fold[:, i * HEAD : (i + 1) * HEAD] for i in range(tiles[j])]
        if tiles[j] > n_chips:
            row = lax.broadcasted_iota(jnp.int32, (rows, HEAD), 0) % ROWS
            edge = spread_rows(tables[0, 8], rows) <= row.astype(F32)
            tile[0] = jnp.where(edge, tile[0], -FAR)
            tile[-1] = jnp.where(edge, tile[-1], -FAR)
        return free, tile

    def finish(j, q, h, free, tile):
        kind = kinds[j]
        mine = slice(h * ROWS, (h + 1) * ROWS)
        short = [t.astype(BF16) for t in tile]
        pens = [jnp.concatenate([(1.0 - k) * FAR, (1.0 - k) * FAR], axis=0).astype(BF16) for k in kind]
        flips = [jnp.concatenate([k * FAR, k * FAR], axis=0).astype(BF16) for k in kind]

        def lower(t, pen):
            return (t.reshape(rows // 16, 16, HEAD) - pen[None]).reshape(rows, HEAD)

        bests = (
            [lower(t, p) for t, p in zip(short, pens)],
            [lower(t, p) for t, p in zip(short, flips)] + [t.astype(BF16) for t in free],
        )
        bases, factors = [], []
        for k in range(2):
            at = slice(k * 2 * ROWS + mine.start, k * 2 * ROWS + mine.stop)
            top = jnp.max(functools.reduce(jnp.maximum, bests[k]).astype(F32), axis=1, keepdims=True) * SCALE
            if start:
                top = jnp.broadcast_to(jnp.maximum(top, NEG), (rows, HEAD))
            else:
                old = olds[j][1][at, :]
                top = jnp.maximum(top, old)
                factors.append(jnp.exp2(old - top))
            bases.append(top)
        low_sum = jnp.zeros((rows, HEAD), F32)
        high_sum = jnp.zeros((rows, HEAD), F32)
        weights = []
        for t, k in zip(tile, kind):
            base = jnp.where(spread_rows(k, rows) > 0, bases[0], bases[1])
            w = jnp.exp2(t * SCALE - base)
            low_sum = low_sum + w * spread_rows(k, rows)
            high_sum = high_sum + w
            weights.append(w.astype(BF16))
        fold = jnp.dot(
            jnp.concatenate(weights, axis=1), values[j, : tiles[j] * HEAD, :], preferred_element_type=F32
        )
        weights = [jnp.exp2(t * SCALE - bases[1]).astype(BF16) for t in free]
        free = jnp.dot(jnp.concatenate(weights, axis=1), low_values[...], preferred_element_type=F32)
        parts = (fold[:, :HEAD], fold[:, HEAD:] + free[:, :HEAD])
        totals = (low_sum, high_sum - low_sum + free[:, HEAD:])
        for k in range(2):
            at = slice(k * 2 * ROWS + mine.start, k * 2 * ROWS + mine.stop)
            place = (k * n_heads + heads.index(h)) * ROWS
            to = slice(place, place + ROWS)
            value, total = parts[k], totals[k]
            if not start:
                value = olds[j][0][at, :] * factors[k] + value
                total = olds[j][2][at, :] * factors[k] + total
            if last:
                total = jnp.broadcast_to(jnp.sum(total, axis=1, keepdims=True), (rows, HEAD))
            if message:
                some = total > 0
                total = jnp.where(some, total, 1.0)
                outs[j][to, :] = (value / total).astype(BF16)
                norms[2 * j + k].append(jnp.where(some, bases[k] + jnp.log2(total), NEG))
            else:
                outs[3 * j][to, :] = value
                outs[3 * j + 1][to, :] = bases[k]
                outs[3 * j + 2][to, :] = total

    ahead = score(*units[0])
    for n, unit in enumerate(units):
        now = ahead
        if n + 1 < len(units):
            ahead = score(*units[n + 1])
        finish(*unit, *now)
    if message:
        for j in range(len(which)):
            pack(outs[j], 2 * n_heads * ROWS, jnp.concatenate(norms[2 * j] + norms[2 * j + 1], axis=0))


def merge(value, top, total, other, norm):
    best = jnp.maximum(top, norm)
    a, b = jnp.exp2(top - best), jnp.exp2(norm - best)
    return value * a + other * b, best, total * a + b


def join(acc, tops, sums, received, *outs):
    for block in range(4):
        rows = slice(block * HEAD, (block + 1) * HEAD)
        norm = unpack(received, 2 * ROWS, block)
        state = merge(acc[rows, :], tops[rows, :], sums[rows, :], received[rows, :].astype(F32), norm)
        outs[0][rows, :], outs[1][rows, :], outs[2][rows, :] = state


def close(tables, mine, mine_tops, mine_sums, received, attended, log_norm):
    flag = tables[0, 9]
    values, norms = [], []
    for block in range(4):
        rows = slice(block * HEAD, (block + 1) * HEAD)
        value, top, total = merge(
            mine[rows, :],
            mine_tops[rows, :],
            mine_sums[rows, :],
            received[rows, :].astype(F32),
            unpack(received, 2 * ROWS, block),
        )
        values.append(value / total)
        norms += to_lanes((top + jnp.log2(total)) * math.log(2.0))
    for slot in range(2):
        for j in range(2):
            low, high = values[j], values[2 + j]
            swap = spread_rows(flag, HEAD) > 0
            pair = (high, low) if slot == 0 else (low, high)
            rows = slice((slot * 2 + j) * HEAD, (slot * 2 + j + 1) * HEAD)
            attended[rows, :] = jnp.where(swap, *pair).astype(BF16)
            pair = (norms[2 + j], norms[j]) if slot == 0 else (norms[j], norms[2 + j])
            log_norm[:, rows] = jnp.where(flag[0:1] > 0, *pair)


def call(body, outs, *args, scalars=0, scratch=(), aliases=None):
    return pl.pallas_call(
        body,
        out_shape=outs,
        in_specs=[pl.BlockSpec(memory_space=pltpu.SMEM if i < scalars else pltpu.VMEM) for i in range(len(args))],
        out_specs=jax.tree.map(lambda _: pl.BlockSpec(memory_space=pltpu.VMEM), outs),
        scratch_shapes=list(scratch),
        input_output_aliases=aliases or {},
        compiler_params=pltpu.CompilerParams(vmem_limit_bytes=40 * 2**20),
        cost_estimate=pl.CostEstimate(flops=1024, bytes_accessed=1024, transcendentals=0),
    )(*args)


def shape(*dims, dtype=F32):
    return jax.ShapeDtypeStruct(dims, dtype)


def attend(chips, which, blocks, ready, state, heads=(0, 1), message=False):
    n, n_chips = len(which), len(chips)
    rows = 2 * len(heads) * ROWS
    outs = [shape(rows + 16, HEAD, dtype=BF16)] * n if message else [shape(rows, HEAD)] * (3 * n)
    wide = n_chips + 1 if chips[0][2] == 0 else n_chips
    return call(
        functools.partial(absorb, chips, which, heads, message),
        outs,
        *blocks,
        *ready,
        *state,
        scratch=[
            pltpu.VMEM((n_chips * HEAD, HEAD), BF16),
            pltpu.VMEM((n_chips * HEAD, 2 * HEAD), BF16),
            pltpu.VMEM((n, wide * HEAD, 2 * HEAD), BF16),
            pltpu.VMEM((n, wide * HEAD, 2 * HEAD), BF16),
        ],
        aliases={len(blocks) + 3 + i: i for i in range(3 * n)} if state and len(heads) == 2 else {},
    )


def get_ready(span_of, place, own, other):
    flags, tables = call(tabulate, [shape(4, 14, 16, HEAD, dtype=BF16), shape(4, 11, 8, HEAD)], span_of, place, scalars=2)
    (both,) = call(arrange, [shape(2, 2 * ROWS, 2 * HEAD, dtype=BF16)], flags, own, other)
    return both, flags, tables


def swap_cores(y, x, c, z):
    return (y, x, 1 - c, z)


def local(queries, keys, values, span_of):
    pb, z = lax.axis_index("pb"), lax.axis_index("ka")
    place = jnp.stack([pb, z]).astype(jnp.int32)

    block = jnp.stack([keys[0], values[0]]).reshape(1, 2, 2, 32, HEAD)
    held = spread(block, along_z)
    held[1], queries = lax.optimization_barrier((held[1], queries))
    shared = jnp.where(pb % 2 == 0, z ^ 1, (z + 7 + 2 * (z % 2)) % 8)
    own = jnp.concatenate([lax.dynamic_slice_in_dim(queries, h * HEAD, HEAD, 1) for h in (z, shared)], axis=1)
    other = send(own, swap_cores)
    ready = get_ready(span_of, place, own, other)
    rows = spread(jnp.concatenate(held, axis=0), along_first)
    rows = [jnp.concatenate(rows[:2], axis=0), jnp.concatenate(rows[2:], axis=0)]
    both, flags, tables = ready
    *rows, flags, tables = lax.optimization_barrier((*rows, flags, tables))
    ready = (both, flags, tables)

    near = [send(half, along_second(STEPS[1])) for half in rows]
    far = [send(half, along_second(STEPS[2])) for half in rows]
    state = attend([(i // 2, i % 2, 0, i) for i in range(4)], (0, 1), rows, ready, ())
    near[0], far[1], *state = lax.optimization_barrier((near[0], far[1], *state))
    across = [send(near[0], along_second(STEPS[2])), send(far[1], along_second(STEPS[1]))]
    chips = [(2 * part + i // 2, i % 2, 1 + part, i) for part in range(2) for i in range(4)]
    state = attend(chips, (0, 1), near + far, ready, state)

    chips = [(i // 2, i % 2, 3, i) for i in range(4)]
    messages = attend(chips, (1, 0), across, ready, state[3:] + state[:3], (1,), True)
    cross, side, *state = lax.optimization_barrier((*messages, *state))
    cross = send(cross, lambda y, x, c, z: (y, x, 1 - c, partner(1 - c, z)))
    side = send(side, lambda y, x, c, z: (y, x, c, partner(c, z)))
    (message,) = attend(chips, (1,), across, ready, state[3:], (0,), True)
    mate = send(message, swap_cores)
    state = attend(chips, (0,), across, ready, state[:3], (0,))
    half = 2 * ROWS
    for message in (cross, side):
        state = call(join, [shape(half, HEAD)] * 3, *state, message)
    return tuple(call(close, [shape(half, HEAD, dtype=BF16), shape(1, half)], tables, *state, mate))


def solution(mesh):
    placed = (P("pb", None), P("ka", "pb", None), P("ka", "pb", None), P())
    return jax.shard_map(
        local, mesh=mesh, in_specs=placed, out_specs=(P("pb", "ka"), P("ka", "pb")), check_vma=False
    )
```
